32 devices in a mesh: ep: 4 (over z), et: 4 (over x, core), rep: 2 (over y).
Axes of the slice: x: 2, y: 2, z: 4, core: 2. Of those that a mesh axis runs over, the one named last changes fastest.
Arguments:
- grad_out: bfloat16 [2048, 7168], P(('ep', 'rep'), 'et'), may hold values from -6 to 6
- combine: float32 [2048, 2], P(('ep', 'rep')), may hold values from 0.1 to 1
- routing: int32 [2048, 2], P(('ep', 'rep')), may hold values from 0 to 3, all different within a row; in each aligned block of 256 rows (0 to 255, 256 to 511, ...) at most 192 rows name the same one
- expert_down_matrix: bfloat16 [4, 7168, 1024], P('ep', 'et'), may hold values from -0.0625 to 0.0625
- gate_pre: bfloat16 [4, 2, 1024, 768], P('ep', 'rep', 'et'), may hold values from -6 to 6
- up_pre: bfloat16 [4, 2, 1024, 768], P('ep', 'rep', 'et'), may hold values from -6 to 6
Outputs:
- grad_gate: bfloat16 [4, 2, 1024, 768], P('ep', 'rep', 'et')
- up_projection_gradient: bfloat16 [4, 2, 1024, 768], P('ep', 'rep', 'et')
- grad_down: bfloat16 [4, 7168, 1024], P('ep', ('et', 'rep'))
The draws below stay inside these ranges and needn't reach their ends.
Inputs may be any that keep to these rules, and one draw needn't show every extreme that they name: `routing`: each row names 2 different experts. Among the 256 rows of one token group (aligned blocks), no expert is named more than 192 times, a bound that some block reaches.
All inputs are finite; a program needn't handle non-finite values.
Results may differ from the reference program's by a relative error of at most 0.015.
Values may be sent and summed in bfloat16 or wider, within the bound.
A program may use at most 64 MiB of HBM per device.

```python
import math
import jax
import jax.numpy as jnp
import numpy as np
from jax import lax

D = 7168
FF = 1024
TOPW = 2
GROUP_TOKENS = 256
CAP = 192
SLOTS = 768
TOKENS = 2048
N_EP = 4
N_ET = 4
N_REP = 2


def block_scale(key, dims, split, low, top_value):
    level = 1.0
    for axis_at, parts in split:
        steps = jax.random.uniform(jax.random.fold_in(jax.random.fold_in(key, 6), axis_at), (parts,), jnp.float32, low / len(split), top_value / len(split))
        level = level * jnp.repeat(jnp.exp(steps), dims[axis_at] // parts).reshape((-1,) + (1,) * (len(dims) - 1 - axis_at))
    return level


def assign_block(stream_key, own, number, rows, count, top, limit, lean):
    order = jax.random.permutation(stream_key, count)
    heavy_load, usual = portions_of(count, rows * top, limit, lean, True), portions_of(count, rows * top, limit, lean, False)
    places = jnp.arange(count)

    def named(lengths, offset_by):
        used = int((lengths > 0).sum())
        fixed = max(1, used // 4)
        passed = fixed + (places - fixed + offset_by * (used - fixed)) % max(1, count - fixed)
        return jnp.zeros((count,), jnp.int32).at[order[jnp.where(places < fixed, places, passed)]].set(jnp.asarray(lengths, jnp.int32))

    lengths = jnp.where(number % 4 == 0, named(heavy_load, number // 4), named(usual, number - number // 4 - 1))
    mixed = jax.random.permutation(jax.random.fold_in(own, 3), count)
    source_of, receiver = mixed[0:count // 2 * 2:2], mixed[1:count // 2 * 2:2]
    room = jnp.minimum(lengths[source_of] - 1, limit - lengths[receiver]) // 2
    room = jnp.where((source_of == order[0]) | (receiver == order[0]) | (lengths[receiver] == 0), 0, jnp.maximum(room, 0))
    passed = jax.random.randint(jax.random.fold_in(own, 4), (count // 2,), 0, 1 << 20) % (room + 1)
    lengths = lengths.at[source_of].add(-passed).at[receiver].add(passed)
    members = jnp.searchsorted(jnp.cumsum(lengths), jnp.arange(rows * top), side="right").astype(jnp.int32)
    listing = members.reshape(top, rows).T
    listing = listing[jax.random.permutation(jax.random.fold_in(own, 1), rows)]
    offset_by = jax.random.randint(jax.random.fold_in(own, 2), (rows, 1), 0, top)
    return jnp.take_along_axis(listing, (jnp.arange(top)[None, :] + offset_by) % top, axis=1)


def portions_of(number_of, total, reach, lean, full):
    weights = [(1 << 20) // math.isqrt(rank ** lean) + 1 for rank in range(1, number_of + 1)]
    largest = reach if full else min(reach, max(-(-total // number_of), total * weights[0] // sum(weights)))
    least = 1 if total - largest >= number_of - 1 else 0
    given, surplus = [largest] + [least] * (number_of - 1), total - largest - least * (number_of - 1)
    while surplus > 0:
        free = [i for i in range(1, number_of) if given[i] < largest] or [i for i in range(1, number_of) if given[i] < reach]
        pool, left = sum([weights[i] for i in free]), surplus
        for i in free:
            addition = min(reach - given[i], max(1, left * weights[i] // pool), surplus)
            given[i] = given[i] + addition
            surplus = surplus - addition
    return np.array(given)


def scatter_about(stream_key, shape, spread, reach, split=(), held_as=jnp.bfloat16):
    array = jax.random.normal(stream_key, shape, jnp.float32) * spread
    if len(split) > 0:
        array = block_scale(stream_key, shape, split, -0.22, 0.18) * array
    return jnp.clip(array, min=-reach, max=reach).astype(held_as)


def setup_inputs(seed: int = 0) -> dict:
    splits = jax.random.split(jax.random.key(seed), 7)
    grad_out = scatter_about(splits[0], (TOKENS, D), 1.0, 6.0, ((0, 8), (1, 4)))
    combine = jnp.clip(jnp.exp(math.log(1.0) - 2.3025851 * jax.random.uniform(splits[1], (TOKENS, TOPW), jnp.float32) ** block_scale(splits[1], (TOKENS, TOPW), ((0, 8),), -0.2, 0.2)), 0.1, 1.0)
    routing_keys = jax.random.split(jax.random.fold_in(splits[2], 1), TOKENS // GROUP_TOKENS)
    routing_turns = jax.random.permutation(jax.random.fold_in(splits[2], 3), TOKENS // GROUP_TOKENS)
    routing = jax.vmap(lambda own, number: assign_block(jax.random.fold_in(splits[2], 2), own, number, GROUP_TOKENS, N_EP, TOPW, CAP, 2))(routing_keys, routing_turns).reshape((TOKENS, TOPW))
    expert_down_matrix = scatter_about(splits[3], (N_EP, D, FF), D ** -0.5, 0.0625, ((0, 4), (1, 4)))
    gate_pre = scatter_about(splits[4], (N_EP, N_REP, FF, SLOTS), 2.0, 6.0, ((0, 4), (1, 2), (2, 4)))
    up_pre = scatter_about(splits[5], (N_EP, N_REP, FF, SLOTS), 1.0, 6.0, ((0, 4), (1, 2), (2, 4)))
    return dict(grad_out=grad_out, combine=combine, routing=routing, expert_down_matrix=expert_down_matrix, gate_pre=gate_pre, up_pre=up_pre)


def reference(grad_out, combine, routing, expert_down_matrix, gate_pre, up_pre):
    groups = N_EP * N_REP
    pair_total = GROUP_TOKENS * TOPW
    pair_ids = routing.reshape(groups, pair_total)
    pair_weights = combine.reshape(groups, pair_total)
    token_rows = grad_out.reshape(groups, GROUP_TOKENS, D)
    slot_iota = jnp.arange(CAP, dtype=jnp.int32)
    pair_iota = jnp.arange(pair_total, dtype=jnp.int32)

    def one_expert(expert):
        is_mine = (pair_ids == expert).astype(jnp.int32)
        ranking = jnp.cumsum(is_mine, axis=1, dtype=jnp.int32) - is_mine
        position = jnp.where(is_mine == 1, ranking, -1)
        matches = position[:, None, :] == slot_iota[None, :, None]
        filled = jnp.any(matches, axis=2)
        pair_index = jnp.sum(jnp.where(matches, pair_iota[None, None, :], 0), axis=2, dtype=jnp.int32)
        token_index = pair_index // TOPW
        routing_pair_weight = jnp.take_along_axis(pair_weights, pair_index, axis=1)
        picked = jax.vmap(lambda block_rows, chosen: jnp.take(block_rows, chosen, axis=0))(token_rows, token_index)
        routed = (picked.astype(jnp.float32) * routing_pair_weight[:, :, None]).astype(jnp.bfloat16)
        routed = jnp.where(filled[:, :, None], routed, jnp.zeros((), jnp.bfloat16))
        routed = routed.reshape(N_EP, N_REP, CAP, D).transpose(1, 0, 2, 3).reshape(N_REP, SLOTS, D)
        down_weight_blocks = expert_down_matrix[expert].reshape(N_ET, D // N_ET, FF).astype(jnp.float32)
        token_row_blocks = routed.reshape(N_REP, SLOTS, N_ET, D // N_ET).astype(jnp.float32)
        partial_value_term = jnp.einsum('kla,egkl->keag', down_weight_blocks, token_row_blocks)
        act_grad = jnp.sum(partial_value_term.astype(jnp.bfloat16).astype(jnp.float32), axis=0)
        gate_activation_values = gate_pre[expert].astype(jnp.float32)
        up_vals = up_pre[expert].astype(jnp.float32)
        gate_sig = jax.nn.sigmoid(gate_activation_values)
        grad_gate = (act_grad * up_vals * gate_sig * (1.0 + gate_activation_values * (1.0 - gate_sig))).astype(jnp.bfloat16)
        up_projection_gradient = (act_grad * gate_activation_values * gate_sig).astype(jnp.bfloat16)
        activation = (gate_activation_values * gate_sig * up_vals).astype(jnp.bfloat16)
        replica_part = jnp.einsum('rsd,rfs->rdf', routed.astype(jnp.float32), activation.astype(jnp.float32))
        grad_down = jnp.sum(replica_part.astype(jnp.bfloat16).astype(jnp.float32), axis=0).astype(jnp.bfloat16)
        return grad_gate, up_projection_gradient, grad_down

    grad_gate, up_projection_gradient, grad_down = lax.map(one_expert, jnp.arange(N_EP, dtype=jnp.int32))
    return (grad_gate, up_projection_gradient, grad_down)
```

```python
import functools

import jax
import jax.numpy as jnp
from jax import lax
from jax.experimental import pallas as pl
from jax.experimental.pallas import tpu as pltpu
from jax.sharding import PartitionSpec as P

MESH = pl.DeviceIdType.MESH
F32 = jnp.float32
BF16 = jnp.bfloat16
AHEAD = (2, 1, 3)


def kernel(
    n_ep, n_et, grad_ref, comb_ref, route_ref, down_ref, gate_ref, up_ref,
    gg_ref, ug_ref, gd_ref,
    out_buf, in_buf, y_buf, weight, act_buf, part_buf, sum_buf, total, coef_g, coef_u, act_grad,
    key_buf, share_buf,
    w_sem, z_send, z_recv, y_send, y_recv, a_send, a_recv, p_send, p_recv,
):
    ep, et, rep = lax.axis_index("ep"), lax.axis_index("et"), lax.axis_index("rep")
    other = 1 - rep
    cap = in_buf.shape[2]
    hidden = gate_ref.shape[0]
    half = in_buf.shape[3]
    across = lax.rem(et + 2, n_et)
    beside = et + 1 - 2 * lax.rem(et, 2)

    def load_w(t):
        return pltpu.make_async_copy(
            down_ref.at[:, pl.ds(t * hidden, hidden)], weight.at[t], w_sem.at[t]
        )

    for t in range(n_et):
        load_w(t).start()

    barrier = pltpu.get_barrier_semaphore()
    for k in range(1, n_ep):
        pl.semaphore_signal(
            barrier, inc=1, device_id={"ep": lax.rem(ep + k, n_ep)}, device_id_type=MESH
        )
    for k in range(1, n_et):
        pl.semaphore_signal(
            barrier, inc=1, device_id={"et": lax.rem(et + k, n_et)}, device_id_type=MESH
        )
    pl.semaphore_signal(barrier, inc=1, device_id={"rep": other}, device_id_type=MESH)

    tokens = grad_ref.shape[0]
    rows = key_buf.shape[0]
    names = lax.broadcasted_iota(jnp.int32, (rows, tokens), 0)
    first = route_ref[0:1, :] == names
    mine = first | (route_ref[1:2, :] == names)
    before = (
        lax.broadcasted_iota(jnp.int32, (tokens, tokens), 0)
        < lax.broadcasted_iota(jnp.int32, (tokens, tokens), 1)
    )
    rank = jnp.dot(
        jnp.where(mine, 1.0, 0.0).astype(BF16),
        jnp.where(before, 1.0, 0.0).astype(BF16),
        preferred_element_type=F32,
    )
    key_buf[...] = jnp.where(mine, rank, -1.0)
    share_buf[...] = jnp.where(first, comb_ref[0:1, :], comb_ref[1:2, :])
    places = lax.broadcasted_iota(jnp.int32, (cap, tokens), 0).astype(F32)

    def pick(expert):
        chosen = key_buf[pl.ds(expert, 1), :] == places
        scale = jnp.sum(
            jnp.where(chosen, share_buf[pl.ds(expert, 1), :], 0.0), axis=1, keepdims=True
        )
        return jnp.where(chosen, 1.0, 0.0).astype(BF16), scale

    def routed(pick_of, h):
        chosen, scale = pick_of
        columns = grad_ref[:, pl.ds(pl.multiple_of(h * half, 128), half)]
        return (jnp.dot(chosen, columns, preferred_element_type=F32) * scale).astype(BF16)

    def z_copy(h, expert, source):
        return pltpu.make_async_remote_copy(
            src_ref=out_buf.at[h, expert],
            dst_ref=in_buf.at[h, source],
            send_sem=z_send.at[h, expert],
            recv_sem=z_recv.at[h, source],
            device_id={"ep": expert},
            device_id_type=MESH,
        )

    def y_copy(h, source):
        return pltpu.make_async_remote_copy(
            src_ref=in_buf.at[h, source],
            dst_ref=y_buf.at[source],
            send_sem=y_send.at[source],
            recv_sem=y_recv.at[source],
            device_id={"rep": other},
            device_id_type=MESH,
        )

    def a_copy(i, r, t, target):
        return pltpu.make_async_remote_copy(
            src_ref=act_buf.at[r, t],
            dst_ref=act_buf.at[r, t],
            send_sem=a_send.at[i],
            recv_sem=a_recv.at[i],
            device_id=target,
            device_id_type=MESH,
        )

    def p_copy(source, t, sender):
        return pltpu.make_async_remote_copy(
            src_ref=part_buf.at[source, t],
            dst_ref=sum_buf.at[source, sender],
            send_sem=p_send.at[source, t],
            recv_sem=p_recv.at[source, sender],
            device_id={"et": t},
            device_id_type=MESH,
        )

    for n, k in enumerate(AHEAD):
        expert = lax.rem(ep + k, n_ep)
        chosen = pick(expert)
        for h in (other, rep):
            out_buf[h, expert] = routed(chosen, h)
        if n == 0:
            pl.semaphore_wait(barrier, n_ep - 1 + n_et - 1 + 1)
        for h in (other, rep):
            z_copy(h, expert, ep).start()
    chosen = pick(ep)
    for h in (other, rep):
        in_buf[h, ep] = routed(chosen, h)
    y_copy(other, ep).start()

    h_value, u_value = gate_ref[...].astype(F32), up_ref[...].astype(F32)
    sig = 1.0 / (1.0 + jnp.exp(-h_value))
    silu = h_value * sig
    coef_g[...] = u_value * sig * (1.0 + h_value * (1.0 - sig))
    coef_u[...] = silu
    act_buf[rep, et] = (silu * u_value).T.astype(BF16)
    to_y, to_x, to_c = {"rep": other}, {"et": across}, {"et": beside}
    a_copy(0, rep, et, to_y).start()
    a_copy(1, rep, et, to_x).start()
    a_copy(3, rep, et, to_c).start()

    for t in range(n_et):
        load_w(t).wait()

    def partial(source):
        def one(k, carry):
            t = lax.rem(et + k, n_et)
            value = jnp.dot(
                in_buf[0, source], weight[t, pl.ds(0, half)], preferred_element_type=F32
            ) + jnp.dot(
                in_buf[1, source], weight[t, pl.ds(half, half)], preferred_element_type=F32
            )
            part_buf[source, t] = value.astype(BF16)

            @pl.when(k < n_et)
            def _():
                p_copy(source, t, et).start()

            return carry

        lax.fori_loop(1, n_et + 1, one, 0)

    def weigh(slots_ref, r, source, start=False):
        turned = slots_ref[...].T
        at = pl.multiple_of(source * cap, 16)
        for t in range(n_et):
            value = jnp.dot(
                turned, act_buf[r, t, pl.ds(at, cap), :], preferred_element_type=F32
            )
            total[t] = value if start else total[t] + value

    partial(ep)
    a_copy(0, other, et, to_y).wait_recv()
    a_copy(2, other, et, to_x).start()
    a_copy(4, other, et, to_c).start()
    a_copy(1, rep, across, to_x).wait_recv()
    a_copy(5, rep, across, to_c).start()
    a_copy(2, other, across, to_x).wait_recv()
    a_copy(6, other, across, to_c).start()
    far = lax.rem(beside + 2, n_et)
    a_copy(3, rep, beside, to_c).wait_recv()
    a_copy(4, other, beside, to_c).wait_recv()
    a_copy(5, rep, far, to_c).wait_recv()
    a_copy(6, other, far, to_c).wait_recv()
    weigh(in_buf.at[rep, ep], rep, ep, True)
    y_copy(other, ep).wait_recv()
    weigh(y_buf.at[ep], other, ep)

    def gather(source):
        value = part_buf[source, et].astype(F32)
        for k in range(1, n_et):
            sender = lax.rem(et + k, n_et)
            p_copy(source, et, sender).wait_recv()
            value = value + sum_buf[source, sender].astype(F32)
        act_grad[pl.ds(pl.multiple_of(source * cap, 16), cap), :] = value

    earlier = ep
    for k in AHEAD:
        source = lax.rem(ep + n_ep - k, n_ep)
        z_copy(other, ep, source).wait_recv()
        y_copy(other, source).start()
        z_copy(rep, ep, source).wait_recv()
        partial(source)
        weigh(in_buf.at[rep, source], rep, source)
        if k != AHEAD[0]:
            y_copy(other, earlier).wait_recv()
            weigh(y_buf.at[earlier], other, earlier)
        gather(earlier)
        earlier = source
    gather(earlier)
    value = act_grad[...].T
    gg_ref[...] = (value * coef_g[...]).astype(BF16)
    ug_ref[...] = (value * coef_u[...]).astype(BF16)
    y_copy(other, earlier).wait_recv()
    weigh(y_buf.at[earlier], other, earlier)
    for t in range(n_et):
        gd_ref[:, pl.ds(t * hidden, hidden)] = total[t].astype(BF16)

    for i, (r, t, target) in enumerate((
        (rep, et, to_y), (rep, et, to_x), (other, et, to_x),
        (rep, et, to_c), (other, et, to_c), (rep, across, to_c), (other, across, to_c),
    )):
        a_copy(i, r, t, target).wait_send()
    for k in range(n_ep):
        source = lax.rem(ep + k, n_ep)
        y_copy(other, source).wait_send()
        if k > 0:
            z_copy(other, source, ep).wait_send()
            z_copy(rep, source, ep).wait_send()
        for j in range(1, n_et):
            p_copy(source, lax.rem(et + j, n_et), et).wait_send()


def fused(n_ep, n_et, grad_out, combine, routing, expert_down_matrix, gate_pre, up_pre):
    tokens, feats = grad_out.shape
    hidden, slots = gate_pre.shape[2:]
    cap, half = slots // n_ep, feats // 2
    vmem = pl.BlockSpec(memory_space=pltpu.VMEM)
    dma = pltpu.SemaphoreType.DMA
    gg, ug, gd = pl.pallas_call(
        functools.partial(kernel, n_ep, n_et),
        out_shape=(
            jax.ShapeDtypeStruct((hidden, slots), BF16),
            jax.ShapeDtypeStruct((hidden, slots), BF16),
            jax.ShapeDtypeStruct((half, n_et * hidden), BF16),
        ),
        in_specs=[vmem, vmem, vmem, pl.BlockSpec(memory_space=pl.ANY), vmem, vmem],
        out_specs=(vmem, vmem, vmem),
        scratch_shapes=[
            pltpu.VMEM((2, n_ep, cap, half), BF16),
            pltpu.VMEM((2, n_ep, cap, half), BF16),
            pltpu.VMEM((n_ep, cap, half), BF16),
            pltpu.VMEM((n_et, feats, hidden), BF16),
            pltpu.VMEM((2, n_et, slots, hidden), BF16),
            pltpu.VMEM((n_ep, n_et, cap, hidden), BF16),
            pltpu.VMEM((n_ep, n_et, cap, hidden), BF16),
            pltpu.VMEM((n_et, half, hidden), F32),
            pltpu.VMEM((hidden, slots), F32),
            pltpu.VMEM((hidden, slots), F32),
            pltpu.VMEM((slots, hidden), F32),
            pltpu.VMEM((16, tokens), F32),
            pltpu.VMEM((16, tokens), F32),
            dma((n_et,)),
            dma((2, n_ep)),
            dma((2, n_ep)),
            dma((n_ep,)),
            dma((n_ep,)),
            dma((7,)),
            dma((7,)),
            dma((n_ep, n_et)),
            dma((n_ep, n_et)),
        ],
        compiler_params=pltpu.CompilerParams(
            collective_id=0, has_side_effects=True, vmem_limit_bytes=50 * 2**20
        ),
    )(grad_out, combine.T, routing.T, expert_down_matrix[0], gate_pre[0, 0], up_pre[0, 0])
    return gg[None, None], ug[None, None], gd[None]


def plain(n_ep, grad_out, combine, routing, expert_down_matrix, gate_pre, up_pre):
    slot_count = gate_pre.shape[-1]
    cap = slot_count // n_ep
    tokens, feats = grad_out.shape
    width = routing.shape[1]
    pairs = tokens * width
    targets = routing.reshape(pairs)
    onehot = targets[:, None] == jnp.arange(n_ep, dtype=jnp.int32)[None, :]
    place = jnp.arange(pairs, dtype=jnp.int32)
    before = (place[None, :] < place[:, None]).astype(BF16)
    counts = jnp.dot(before, onehot.astype(BF16), preferred_element_type=F32)
    ranking = jnp.sum(jnp.where(onehot, counts, 0.0), axis=1).astype(jnp.int32)
    destination = targets * cap + ranking
    matches = destination[None, :] == jnp.arange(slot_count, dtype=jnp.int32)[:, None]
    filled = jnp.any(matches, axis=1)
    source = jnp.sum(jnp.where(matches, place[None, :], 0), axis=1, dtype=jnp.int32)
    scale = jnp.take(combine.reshape(pairs), source)
    rows = jnp.take(grad_out, source // width, axis=0).astype(F32)
    outgoing = jnp.where(filled[:, None], (rows * scale[:, None]).astype(BF16), jnp.zeros((), BF16))
    incoming = lax.all_to_all(
        outgoing.reshape(n_ep, cap, feats), "ep", split_axis=0, concat_axis=0, tiled=True
    ).reshape(slot_count, feats)
    act_grad = lax.psum_scatter(
        lax.dot_general(
            expert_down_matrix[0], incoming, (((0,), (1,)), ((), ())), preferred_element_type=F32
        ).astype(BF16),
        "et",
        scatter_dimension=0,
        tiled=True,
    ).astype(F32)
    h, u = gate_pre[0, 0].astype(F32), up_pre[0, 0].astype(F32)
    sig = jax.nn.sigmoid(h)
    grad_gate = (act_grad * u * sig * (1.0 + h * (1.0 - sig))).astype(BF16)
    up_grad = (act_grad * h * sig).astype(BF16)
    activation = (h * sig * u).astype(BF16)
    part = lax.dot_general(
        incoming,
        lax.all_gather(activation, "et", axis=0, tiled=True),
        (((0,), (1,)), ((), ())),
        preferred_element_type=F32,
    ).astype(BF16)
    grad_down = lax.psum_scatter(part, "rep", scatter_dimension=0, tiled=True)
    return grad_gate[None, None], up_grad[None, None], grad_down[None]


def solution(mesh):
    n_ep, n_et, n_rep = mesh.shape["ep"], mesh.shape["et"], mesh.shape["rep"]

    def local(grad_out, combine, routing, expert_down_matrix, gate_pre, up_pre):
        args = (grad_out, combine, routing, expert_down_matrix, gate_pre, up_pre)
        whole_tiles = gate_pre.shape[-1] // n_ep % 16 == 0
        if n_ep == 4 and n_et == 4 and n_rep == 2 and whole_tiles:
            return fused(n_ep, n_et, *args)
        return plain(n_ep, *args)

    return jax.shard_map(
        local,
        mesh=mesh,
        in_specs=(
            P(("ep", "rep"), "et"),
            P(("ep", "rep"), None),
            P(("ep", "rep"), None),
            P("ep", "et", None),
            P("ep", "rep", "et", None),
            P("ep", "rep", "et", None),
        ),
        out_specs=(
            P("ep", "rep", "et", None),
            P("ep", "rep", "et", None),
            P("ep", ("et", "rep"), None),
        ),
        check_vma=False,
    )
```

```python
import functools

import jax
import jax.numpy as jnp
from jax import lax
from jax.experimental import pallas as pl
from jax.experimental.pallas import tpu as pltpu
from jax.sharding import PartitionSpec as P

MESH = pl.DeviceIdType.MESH
F32 = jnp.float32
BF16 = jnp.bfloat16


def kernel(
    n_ep, n_et, grad_hbm, comb_hbm, route_hbm, down_ref, gate_hbm, up_hbm,
    gg_ref, ug_ref, gd_ref,
    tok_buf, meta_buf, out_buf, in_buf, y_buf, weight, act_buf, part_buf, sum_buf, total,
    coef_g, coef_u, act_grad, comb_ref, route_ref, gate_ref, up_ref,
    w_sem, l_sem, t_send, t_recv, m_send, m_recv,
    z_send, z_recv, y_send, y_recv, a_send, a_recv, p_send, p_recv,
):
    ep, et, rep = lax.axis_index("ep"), lax.axis_index("et"), lax.axis_index("rep")
    other = 1 - rep
    cap, half = in_buf.shape[2:]
    tokens = tok_buf.shape[2]
    hidden = gate_ref.shape[0]
    across = lax.rem(et + 2, n_et)
    beside = et + 1 - 2 * lax.rem(et, 2)
    last = n_ep - 1
    near = ep + 1 - 2 * lax.rem(ep, 2)
    inner = lax.rem((ep + 1) // 2, 2)
    is_inner = inner == 1
    second = inner * (last - ep) + (1 - inner) * (last - near)
    third = inner * (last - near) + (1 - inner) * (last - ep)
    onward = inner * (last - ep) + (1 - inner) * near

    def load(i):
        if i < 2:
            h = (other, rep)[i]
            columns = pl.ds(pl.multiple_of(h * half, 128), half)
            return pltpu.make_async_copy(grad_hbm.at[:, columns], tok_buf.at[ep, h], l_sem.at[i])
        source, target = (
            (comb_hbm, comb_ref), (route_hbm, route_ref), (gate_hbm, gate_ref), (up_hbm, up_ref)
        )[i - 2]
        return pltpu.make_async_copy(source, target, l_sem.at[i])

    def load_w(t):
        return pltpu.make_async_copy(
            down_ref.at[:, pl.ds(t * hidden, hidden)], weight.at[t], w_sem.at[t]
        )

    barrier = pltpu.get_barrier_semaphore()
    for k in range(1, n_ep):
        pl.semaphore_signal(
            barrier, inc=1, device_id={"ep": lax.rem(ep + k, n_ep)}, device_id_type=MESH
        )
    for k in range(1, n_et):
        pl.semaphore_signal(
            barrier, inc=1, device_id={"et": lax.rem(et + k, n_et)}, device_id_type=MESH
        )
    pl.semaphore_signal(barrier, inc=1, device_id={"rep": other}, device_id_type=MESH)
    for i in (2, 3, 0, 1, 4, 5):
        load(i).start()
    for t in range(n_et):
        load_w(t).start()

    def t_copy(source, h):
        return pltpu.make_async_remote_copy(
            src_ref=tok_buf.at[source, h],
            dst_ref=tok_buf.at[source, h],
            send_sem=t_send.at[source, h],
            recv_sem=t_recv.at[source, h],
            device_id={"ep": onward},
            device_id_type=MESH,
        )

    def m_copy(source):
        return pltpu.make_async_remote_copy(
            src_ref=meta_buf.at[source],
            dst_ref=meta_buf.at[source],
            send_sem=m_send.at[source],
            recv_sem=m_recv.at[source],
            device_id={"ep": onward},
            device_id_type=MESH,
        )

    def z_copy(source, h):
        return pltpu.make_async_remote_copy(
            src_ref=out_buf.at[h, source],
            dst_ref=in_buf.at[h, source],
            send_sem=z_send.at[h, source],
            recv_sem=z_recv.at[h, source],
            device_id={"ep": near},
            device_id_type=MESH,
        )

    def y_copy(source):
        return pltpu.make_async_remote_copy(
            src_ref=in_buf.at[other, source],
            dst_ref=y_buf.at[source],
            send_sem=y_send.at[source],
            recv_sem=y_recv.at[source],
            device_id={"rep": other},
            device_id_type=MESH,
        )

    def a_copy(i, r, t, target):
        return pltpu.make_async_remote_copy(
            src_ref=act_buf.at[r, t],
            dst_ref=act_buf.at[r, t],
            send_sem=a_send.at[i],
            recv_sem=a_recv.at[i],
            device_id=target,
            device_id_type=MESH,
        )

    def p_copy(source, t, sender):
        return pltpu.make_async_remote_copy(
            src_ref=part_buf.at[source, t],
            dst_ref=sum_buf.at[source, sender],
            send_sem=p_send.at[source, t],
            recv_sem=p_recv.at[source, sender],
            device_id={"et": t},
            device_id_type=MESH,
        )

    load(2).wait()
    load(3).wait()
    rows = meta_buf.shape[2]
    names = lax.broadcasted_iota(jnp.int32, (rows, tokens), 0)
    first = route_ref[0:1, :] == names
    mine = first | (route_ref[1:2, :] == names)
    before = (
        lax.broadcasted_iota(jnp.int32, (tokens, tokens), 0)
        < lax.broadcasted_iota(jnp.int32, (tokens, tokens), 1)
    )
    rank = jnp.dot(
        jnp.where(mine, 1.0, 0.0).astype(BF16),
        jnp.where(before, 1.0, 0.0).astype(BF16),
        preferred_element_type=F32,
    )
    meta_buf[ep, 0] = jnp.where(mine, rank, -1.0)
    meta_buf[ep, 1] = jnp.where(first, comb_ref[0:1, :], comb_ref[1:2, :])
    places = lax.broadcasted_iota(jnp.int32, (cap, tokens), 0).astype(F32)

    def routed(source, h, expert):
        chosen = meta_buf[source, 0, pl.ds(expert, 1), :] == places
        scale = jnp.sum(
            jnp.where(chosen, meta_buf[source, 1, pl.ds(expert, 1), :], 0.0),
            axis=1,
            keepdims=True,
        )
        picked = jnp.dot(
            jnp.where(chosen, 1.0, 0.0).astype(BF16),
            tok_buf[source, h],
            preferred_element_type=F32,
        )
        return (picked * scale).astype(BF16)

    pl.semaphore_wait(barrier, n_ep - 1 + n_et - 1 + 1)
    m_copy(ep).start()
    for i, h in enumerate((other, rep)):
        load(i).wait()
        t_copy(ep, h).start()

    def pass_slots(source, h):
        out_buf[h, source] = routed(source, h, near)
        z_copy(source, h).start()

    @pl.when(is_inner)
    def _():
        for h in (other, rep):
            pass_slots(ep, h)

    in_buf[other, ep] = routed(ep, other, ep)
    y_copy(ep).start()
    in_buf[rep, ep] = routed(ep, rep, ep)

    load(4).wait()
    load(5).wait()
    h_value, u_value = gate_ref[...].astype(F32), up_ref[...].astype(F32)
    sig = 1.0 / (1.0 + jnp.exp(-h_value))
    silu = h_value * sig
    act_buf[rep, et] = (silu * u_value).T.astype(BF16)
    to_y, to_x, to_c = {"rep": other}, {"et": across}, {"et": beside}
    a_copy(0, rep, et, to_y).start()
    a_copy(1, rep, et, to_x).start()
    a_copy(3, rep, et, to_c).start()
    coef_g[...] = u_value * sig * (1.0 + h_value * (1.0 - sig))
    coef_u[...] = silu

    def partial(source):
        def one(k, carry):
            t = lax.rem(et + k, n_et)
            value = jnp.dot(
                in_buf[0, source], weight[t, pl.ds(0, half)], preferred_element_type=F32
            ) + jnp.dot(
                in_buf[1, source], weight[t, pl.ds(half, half)], preferred_element_type=F32
            )
            part_buf[source, t] = value.astype(BF16)

            @pl.when(k < n_et)
            def _():
                p_copy(source, t, et).start()

            return carry

        lax.fori_loop(1, n_et + 1, one, 0)

    def weigh(slots_ref, r, source, start=False):
        turned = slots_ref[...].T
        at = pl.multiple_of(source * cap, 16)
        for t in range(n_et):
            value = jnp.dot(
                turned, act_buf[r, t, pl.ds(at, cap), :], preferred_element_type=F32
            )
            total[t] = value if start else total[t] + value

    def weigh_own(source, start=False):
        weigh(in_buf.at[rep, source], rep, source, start)

    def weigh_y(source):
        y_copy(source).wait_recv()
        weigh(y_buf.at[source], other, source)

    def gather(source):
        value = part_buf[source, et].astype(F32)
        for k in range(1, n_et):
            sender = lax.rem(et + k, n_et)
            p_copy(source, et, sender).wait_recv()
            value = value + sum_buf[source, sender].astype(F32)
        act_grad[pl.ds(pl.multiple_of(source * cap, 16), cap), :] = value

    def arrive(which, h):
        source = (near, second, third)[which]

        @pl.when(is_inner)
        def _():
            if h is other:
                m_copy(source).wait_recv()
            t_copy(source, h).wait_recv()
            if which == 0:
                if h is other:
                    m_copy(source).start()
                t_copy(source, h).start()
            else:
                pass_slots(source, h)
            in_buf[h, source] = routed(source, h, ep)

        @pl.when(inner == 0)
        def _():
            z_copy(source, h).wait_recv()

        if h is other:
            y_copy(source).start()

    for t in range(n_et):
        load_w(t).wait()
    partial(ep)
    arrive(0, other)
    a_copy(0, other, et, to_y).wait_recv()
    a_copy(2, other, et, to_x).start()
    a_copy(4, other, et, to_c).start()
    a_copy(1, rep, across, to_x).wait_recv()
    a_copy(5, rep, across, to_c).start()
    arrive(1, other)
    gather(ep)
    arrive(0, rep)
    a_copy(2, other, across, to_x).wait_recv()
    a_copy(6, other, across, to_c).start()
    partial(near)
    arrive(1, rep)
    partial(second)
    far = lax.rem(beside + 2, n_et)
    a_copy(3, rep, beside, to_c).wait_recv()
    a_copy(4, other, beside, to_c).wait_recv()
    a_copy(5, rep, far, to_c).wait_recv()
    a_copy(6, other, far, to_c).wait_recv()
    weigh_own(ep, True)
    weigh_y(ep)
    weigh_own(near)
    gather(near)
    arrive(2, other)
    weigh_y(near)
    weigh_own(second)
    gather(second)
    arrive(2, rep)
    partial(third)
    weigh_y(second)
    weigh_own(third)
    weigh_y(third)
    for t in range(n_et):
        gd_ref[:, pl.ds(t * hidden, hidden)] = total[t].astype(BF16)
    gather(third)
    value = act_grad[...].T
    gg_ref[...] = (value * coef_g[...]).astype(BF16)
    ug_ref[...] = (value * coef_u[...]).astype(BF16)

    for i, (r, t, target) in enumerate((
        (rep, et, to_y), (rep, et, to_x), (other, et, to_x),
        (rep, et, to_c), (other, et, to_c), (rep, across, to_c), (other, across, to_c),
    )):
        a_copy(i, r, t, target).wait_send()
    m_copy(ep).wait_send()
    for h in (other, rep):
        t_copy(ep, h).wait_send()

    @pl.when(is_inner)
    def _():
        m_copy(near).wait_send()
        for h in (other, rep):
            t_copy(near, h).wait_send()
            for source in (ep, second, third):
                z_copy(source, h).wait_send()

    for source in (ep, near, second, third):
        y_copy(source).wait_send()
        for j in range(1, n_et):
            p_copy(source, lax.rem(et + j, n_et), et).wait_send()


def fused(n_ep, n_et, grad_out, combine, routing, expert_down_matrix, gate_pre, up_pre):
    tokens, feats = grad_out.shape
    hidden, slots = gate_pre.shape[2:]
    cap, half = slots // n_ep, feats // 2
    width = routing.shape[1]
    vmem = pl.BlockSpec(memory_space=pltpu.VMEM)
    dma = pltpu.SemaphoreType.DMA
    gg, ug, gd = pl.pallas_call(
        functools.partial(kernel, n_ep, n_et),
        out_shape=(
            jax.ShapeDtypeStruct((hidden, slots), BF16),
            jax.ShapeDtypeStruct((hidden, slots), BF16),
            jax.ShapeDtypeStruct((half, n_et * hidden), BF16),
        ),
        in_specs=[pl.BlockSpec(memory_space=pltpu.HBM)] * 6,
        out_specs=(vmem, vmem, vmem),
        scratch_shapes=[
            pltpu.VMEM((n_ep, 2, tokens, half), BF16),
            pltpu.VMEM((n_ep, 2, 8, tokens), F32),
            pltpu.VMEM((2, n_ep, cap, half), BF16),
            pltpu.VMEM((2, n_ep, cap, half), BF16),
            pltpu.VMEM((n_ep, cap, half), BF16),
            pltpu.VMEM((n_et, feats, hidden), BF16),
            pltpu.VMEM((2, n_et, slots, hidden), BF16),
            pltpu.VMEM((n_ep, n_et, cap, hidden), BF16),
            pltpu.VMEM((n_ep, n_et, cap, hidden), BF16),
            pltpu.VMEM((n_et, half, hidden), F32),
            pltpu.VMEM((hidden, slots), F32),
            pltpu.VMEM((hidden, slots), F32),
            pltpu.VMEM((slots, hidden), F32),
            pltpu.VMEM((width, tokens), F32),
            pltpu.VMEM((width, tokens), jnp.int32),
            pltpu.VMEM((hidden, slots), BF16),
            pltpu.VMEM((hidden, slots), BF16),
            dma((n_et,)),
            dma((6,)),
            dma((n_ep, 2)),
            dma((n_ep, 2)),
            dma((n_ep,)),
            dma((n_ep,)),
            dma((2, n_ep)),
            dma((2, n_ep)),
            dma((n_ep,)),
            dma((n_ep,)),
            dma((7,)),
            dma((7,)),
            dma((n_ep, n_et)),
            dma((n_ep, n_et)),
        ],
        compiler_params=pltpu.CompilerParams(
            collective_id=0, has_side_effects=True, vmem_limit_bytes=60 * 2**20
        ),
    )(grad_out, combine.T, routing.T, expert_down_matrix[0], gate_pre[0, 0], up_pre[0, 0])
    return gg[None, None], ug[None, None], gd[None]


def plain(n_ep, grad_out, combine, routing, expert_down_matrix, gate_pre, up_pre):
    slot_count = gate_pre.shape[-1]
    cap = slot_count // n_ep
    tokens, feats = grad_out.shape
    width = routing.shape[1]
    pairs = tokens * width
    targets = routing.reshape(pairs)
    onehot = targets[:, None] == jnp.arange(n_ep, dtype=jnp.int32)[None, :]
    place = jnp.arange(pairs, dtype=jnp.int32)
    before = (place[None, :] < place[:, None]).astype(BF16)
    counts = jnp.dot(before, onehot.astype(BF16), preferred_element_type=F32)
    ranking = jnp.sum(jnp.where(onehot, counts, 0.0), axis=1).astype(jnp.int32)
    destination = targets * cap + ranking
    matches = destination[None, :] == jnp.arange(slot_count, dtype=jnp.int32)[:, None]
    filled = jnp.any(matches, axis=1)
    source = jnp.sum(jnp.where(matches, place[None, :], 0), axis=1, dtype=jnp.int32)
    scale = jnp.take(combine.reshape(pairs), source)
    rows = jnp.take(grad_out, source // width, axis=0).astype(F32)
    outgoing = jnp.where(filled[:, None], (rows * scale[:, None]).astype(BF16), jnp.zeros((), BF16))
    incoming = lax.all_to_all(
        outgoing.reshape(n_ep, cap, feats), "ep", split_axis=0, concat_axis=0, tiled=True
    ).reshape(slot_count, feats)
    act_grad = lax.psum_scatter(
        lax.dot_general(
            expert_down_matrix[0], incoming, (((0,), (1,)), ((), ())), preferred_element_type=F32
        ).astype(BF16),
        "et",
        scatter_dimension=0,
        tiled=True,
    ).astype(F32)
    h, u = gate_pre[0, 0].astype(F32), up_pre[0, 0].astype(F32)
    sig = jax.nn.sigmoid(h)
    grad_gate = (act_grad * u * sig * (1.0 + h * (1.0 - sig))).astype(BF16)
    up_grad = (act_grad * h * sig).astype(BF16)
    activation = (h * sig * u).astype(BF16)
    part = lax.dot_general(
        incoming,
        lax.all_gather(activation, "et", axis=0, tiled=True),
        (((0,), (1,)), ((), ())),
        preferred_element_type=F32,
    ).astype(BF16)
    grad_down = lax.psum_scatter(part, "rep", scatter_dimension=0, tiled=True)
    return grad_gate[None, None], up_grad[None, None], grad_down[None]


def solution(mesh):
    n_ep, n_et, n_rep = mesh.shape["ep"], mesh.shape["et"], mesh.shape["rep"]

    def local(grad_out, combine, routing, expert_down_matrix, gate_pre, up_pre):
        args = (grad_out, combine, routing, expert_down_matrix, gate_pre, up_pre)
        whole_tiles = gate_pre.shape[-1] // n_ep % 16 == 0
        if n_ep == 4 and n_et == 4 and n_rep == 2 and whole_tiles:
            return fused(n_ep, n_et, *args)
        return plain(n_ep, *args)

    return jax.shard_map(
        local,
        mesh=mesh,
        in_specs=(
            P(("ep", "rep"), "et"),
            P(("ep", "rep"), None),
            P(("ep", "rep"), None),
            P("ep", "et", None),
            P("ep", "rep", "et", None),
            P("ep", "rep", "et", None),
        ),
        out_specs=(
            P("ep", "rep", "et", None),
            P("ep", "rep", "et", None),
            P("ep", ("et", "rep"), None),
        ),
        check_vma=False,
    )
```

```python
import functools

import jax
import jax.numpy as jnp
from jax import lax
from jax.experimental import pallas as pl
from jax.experimental.pallas import tpu as pltpu
from jax.sharding import PartitionSpec as P

MESH = pl.DeviceIdType.MESH
F32 = jnp.float32
BF16 = jnp.bfloat16


def kernel(
    n_ep, n_et, grad_hbm, comb_hbm, route_hbm, down_ref, gate_hbm, up_hbm,
    gg_ref, ug_ref, gd_ref,
    tok_buf, meta_buf, out_buf, in_buf, y_buf, weight, act_buf, part_buf, sum_buf, total,
    coef_g, coef_u, act_grad, begun, comb_ref, route_ref, gate_ref, up_ref,
    w_sem, l_sem, t_send, t_recv, c_send, c_recv, m_send, m_recv,
    z_send, z_recv, y_send, y_recv, a_send, a_recv, p_send, p_recv,
):
    ep, et, rep = lax.axis_index("ep"), lax.axis_index("et"), lax.axis_index("rep")
    other = 1 - rep
    cap, half = in_buf.shape[2:]
    tokens = tok_buf.shape[2]
    hidden = gate_ref.shape[0]
    across = lax.rem(et + 2, n_et)
    beside = et + 1 - 2 * lax.rem(et, 2)
    last = n_ep - 1
    near = ep + 1 - 2 * lax.rem(ep, 2)
    inner = lax.rem((ep + 1) // 2, 2)
    is_inner = inner == 1
    second = inner * (last - ep) + (1 - inner) * (last - near)
    third = inner * (last - near) + (1 - inner) * (last - ep)
    onward = inner * (last - ep) + (1 - inner) * near

    def load(i):
        if i < 2:
            h = (other, rep)[i]
            columns = pl.ds(pl.multiple_of(h * half, 128), half)
            return pltpu.make_async_copy(grad_hbm.at[:, columns], tok_buf.at[ep, h], l_sem.at[i])
        source, target = (
            (comb_hbm, comb_ref), (route_hbm, route_ref), (gate_hbm, gate_ref), (up_hbm, up_ref)
        )[i - 2]
        return pltpu.make_async_copy(source, target, l_sem.at[i])

    def load_w(t):
        return pltpu.make_async_copy(
            down_ref.at[:, pl.ds(t * hidden, hidden)], weight.at[t], w_sem.at[t]
        )

    barrier = pltpu.get_barrier_semaphore()
    for k in range(1, n_ep):
        pl.semaphore_signal(
            barrier, inc=1, device_id={"ep": lax.rem(ep + k, n_ep)}, device_id_type=MESH
        )
    for k in range(1, n_et):
        pl.semaphore_signal(
            barrier, inc=1, device_id={"et": lax.rem(et + k, n_et)}, device_id_type=MESH
        )
    pl.semaphore_signal(barrier, inc=1, device_id={"rep": other}, device_id_type=MESH)
    for i in (0, 1, 2, 3, 4, 5):
        load(i).start()
    for t in range(n_et):
        load_w(t).start()

    def t_copy(source, h):
        return pltpu.make_async_remote_copy(
            src_ref=tok_buf.at[source, h],
            dst_ref=tok_buf.at[source, h],
            send_sem=t_send.at[source, h],
            recv_sem=t_recv.at[source, h],
            device_id={"ep": onward},
            device_id_type=MESH,
        )

    cuts = (pl.ds(0, half // 256 * 128 + 128), pl.ds(half // 256 * 128 + 128, half - half // 256 * 128 - 128))

    def t_piece(source, j):
        piece = tok_buf.at[source, rep, :, cuts[j]]
        return pltpu.make_async_remote_copy(
            src_ref=piece,
            dst_ref=piece,
            send_sem=c_send.at[j],
            recv_sem=c_recv.at[j],
            device_id={"ep": onward},
            device_id_type=MESH,
        )

    def z_piece(source, j):
        return pltpu.make_async_remote_copy(
            src_ref=out_buf.at[rep, source, :, cuts[j]],
            dst_ref=in_buf.at[rep, source, :, cuts[j]],
            send_sem=c_send.at[2 + j],
            recv_sem=c_recv.at[2 + j],
            device_id={"ep": near},
            device_id_type=MESH,
        )

    def m_copy(source):
        return pltpu.make_async_remote_copy(
            src_ref=meta_buf.at[source],
            dst_ref=meta_buf.at[source],
            send_sem=m_send.at[source],
            recv_sem=m_recv.at[source],
            device_id={"ep": onward},
            device_id_type=MESH,
        )

    def z_copy(source, h):
        return pltpu.make_async_remote_copy(
            src_ref=out_buf.at[h, source],
            dst_ref=in_buf.at[h, source],
            send_sem=z_send.at[h, source],
            recv_sem=z_recv.at[h, source],
            device_id={"ep": near},
            device_id_type=MESH,
        )

    def y_copy(source):
        return pltpu.make_async_remote_copy(
            src_ref=in_buf.at[other, source],
            dst_ref=y_buf.at[source],
            send_sem=y_send.at[source],
            recv_sem=y_recv.at[source],
            device_id={"rep": other},
            device_id_type=MESH,
        )

    def a_copy(i, r, t, target):
        return pltpu.make_async_remote_copy(
            src_ref=act_buf.at[r, t],
            dst_ref=act_buf.at[r, t],
            send_sem=a_send.at[i],
            recv_sem=a_recv.at[i],
            device_id=target,
            device_id_type=MESH,
        )

    def p_copy(source, t, sender):
        return pltpu.make_async_remote_copy(
            src_ref=part_buf.at[source, t],
            dst_ref=sum_buf.at[source, sender],
            send_sem=p_send.at[source, t],
            recv_sem=p_recv.at[source, sender],
            device_id={"et": t},
            device_id_type=MESH,
        )

    pl.semaphore_wait(barrier, n_ep - 1 + n_et - 1 + 1)
    for i, h in enumerate((other, rep)):
        load(i).wait()
        t_copy(ep, h).start()

    load(2).wait()
    load(3).wait()
    rows = meta_buf.shape[2]
    names = lax.broadcasted_iota(jnp.int32, (rows, tokens), 0)
    first = route_ref[0:1, :] == names
    mine = first | (route_ref[1:2, :] == names)
    before = (
        lax.broadcasted_iota(jnp.int32, (tokens, tokens), 0)
        < lax.broadcasted_iota(jnp.int32, (tokens, tokens), 1)
    )
    rank = jnp.dot(
        jnp.where(mine, 1.0, 0.0).astype(BF16),
        jnp.where(before, 1.0, 0.0).astype(BF16),
        preferred_element_type=F32,
    )
    meta_buf[ep, 0] = jnp.where(mine, rank, -1.0)
    meta_buf[ep, 1] = jnp.where(first, comb_ref[0:1, :], comb_ref[1:2, :])
    places = lax.broadcasted_iota(jnp.int32, (cap, tokens), 0).astype(F32)

    def routed(source, h, expert, columns=slice(None)):
        chosen = meta_buf[source, 0, pl.ds(expert, 1), :] == places
        scale = jnp.sum(
            jnp.where(chosen, meta_buf[source, 1, pl.ds(expert, 1), :], 0.0),
            axis=1,
            keepdims=True,
        )
        picked = jnp.dot(
            jnp.where(chosen, 1.0, 0.0).astype(BF16),
            tok_buf[source, h, :, columns],
            preferred_element_type=F32,
        )
        return (picked * scale).astype(BF16)

    m_copy(ep).start()

    def pass_slots(source, h):
        out_buf[h, source] = routed(source, h, near)
        z_copy(source, h).start()

    @pl.when(is_inner)
    def _():
        for h in (other, rep):
            pass_slots(ep, h)

    in_buf[other, ep] = routed(ep, other, ep)
    y_copy(ep).start()
    in_buf[rep, ep] = routed(ep, rep, ep)

    load(4).wait()
    load(5).wait()
    h_value, u_value = gate_ref[...].astype(F32), up_ref[...].astype(F32)
    sig = 1.0 / (1.0 + jnp.exp(-h_value))
    silu = h_value * sig
    act_buf[rep, et] = (silu * u_value).T.astype(BF16)
    to_y, to_x, to_c = {"rep": other}, {"et": across}, {"et": beside}
    a_copy(0, rep, et, to_y).start()
    a_copy(1, rep, et, to_x).start()
    a_copy(3, rep, et, to_c).start()
    coef_g[...] = u_value * sig * (1.0 + h_value * (1.0 - sig))
    coef_u[...] = silu

    def product(h, source, t):
        return jnp.dot(
            in_buf[h, source],
            weight[t, pl.ds(pl.multiple_of(h * half, 128), half)],
            preferred_element_type=F32,
        )

    def begin(source):
        def one(t, carry):
            begun[t] = product(other, source, t)
            return carry

        lax.fori_loop(0, n_et, one, 0)

    def partial(source, is_begun=False):
        def one(k, carry):
            base = et + lax.rem((k + 1) // 2, 2) * (beside - et)
            t = lax.rem(base + 2 * (1 - k // 2), n_et)
            value = product(rep, source, t)
            value = value + (begun[t] if is_begun else product(other, source, t))
            part_buf[source, t] = value.astype(BF16)

            @pl.when(k < n_et - 1)
            def _():
                p_copy(source, t, et).start()

            return carry

        lax.fori_loop(0, n_et, one, 0)

    def weigh(slots_ref, r, source, start=False):
        turned = slots_ref[...].T
        at = pl.multiple_of(source * cap, 16)
        for t in range(n_et):
            value = jnp.dot(
                turned, act_buf[r, t, pl.ds(at, cap), :], preferred_element_type=F32
            )
            total[t] = value if start else total[t] + value

    def weigh_own(source, start=False):
        weigh(in_buf.at[rep, source], rep, source, start)

    def weigh_y(source):
        y_copy(source).wait_recv()
        weigh(y_buf.at[source], other, source)

    def gather(source):
        value = part_buf[source, et].astype(F32)
        for k in range(1, n_et):
            sender = lax.rem(et + k, n_et)
            p_copy(source, et, sender).wait_recv()
            value = value + sum_buf[source, sender].astype(F32)
        act_grad[pl.ds(pl.multiple_of(source * cap, 16), cap), :] = value

    def arrive(which, h):
        source = (near, second, third)[which]

        @pl.when(is_inner)
        def _():
            if h is other:
                m_copy(source).wait_recv()
            t_copy(source, h).wait_recv()
            if which == 0:
                if h is other:
                    m_copy(source).start()
                    t_copy(source, h).start()
                else:
                    for j in range(2):
                        t_piece(source, j).start()
            else:
                pass_slots(source, h)
            in_buf[h, source] = routed(source, h, ep)

        @pl.when(inner == 0)
        def _():
            z_copy(source, h).wait_recv()

        if h is other:
            y_copy(source).start()

    def arrive_last():
        @pl.when(is_inner)
        def _():
            for j in range(2):
                t_piece(third, j).wait_recv()
                out_buf[rep, third, :, cuts[j]] = routed(third, rep, near, cuts[j])
                z_piece(third, j).start()
            in_buf[rep, third] = routed(third, rep, ep)

        @pl.when(inner == 0)
        def _():
            for j in range(2):
                z_piece(third, j).wait_recv()

    for t in range(n_et):
        load_w(t).wait()
    partial(ep)
    arrive(0, other)
    a_copy(0, other, et, to_y).wait_recv()
    a_copy(2, other, et, to_x).start()
    a_copy(4, other, et, to_c).start()
    a_copy(1, rep, across, to_x).wait_recv()
    a_copy(5, rep, across, to_c).start()
    arrive(1, other)
    gather(ep)
    arrive(0, rep)
    a_copy(2, other, across, to_x).wait_recv()
    a_copy(6, other, across, to_c).start()
    partial(near)
    arrive(1, rep)
    partial(second)
    far = lax.rem(beside + 2, n_et)
    a_copy(3, rep, beside, to_c).wait_recv()
    a_copy(4, other, beside, to_c).wait_recv()
    a_copy(5, rep, far, to_c).wait_recv()
    a_copy(6, other, far, to_c).wait_recv()
    weigh_own(ep, True)
    weigh_y(ep)
    weigh_own(near)
    gather(near)
    arrive(2, other)
    weigh_y(near)
    weigh_own(second)
    gather(second)
    begin(third)
    arrive_last()
    partial(third, True)
    weigh_y(second)
    weigh_own(third)
    weigh_y(third)
    for t in range(n_et):
        gd_ref[:, pl.ds(t * hidden, hidden)] = total[t].astype(BF16)
    gather(third)
    value = act_grad[...].T
    gg_ref[...] = (value * coef_g[...]).astype(BF16)
    ug_ref[...] = (value * coef_u[...]).astype(BF16)

    for i, (r, t, target) in enumerate((
        (rep, et, to_y), (rep, et, to_x), (other, et, to_x),
        (rep, et, to_c), (other, et, to_c), (rep, across, to_c), (other, across, to_c),
    )):
        a_copy(i, r, t, target).wait_send()
    m_copy(ep).wait_send()
    for h in (other, rep):
        t_copy(ep, h).wait_send()

    @pl.when(is_inner)
    def _():
        m_copy(near).wait_send()
        for h in (other, rep):
            for source in (ep, second):
                z_copy(source, h).wait_send()
        t_copy(near, other).wait_send()
        z_copy(third, other).wait_send()
        for j in range(2):
            t_piece(near, j).wait_send()
            z_piece(third, j).wait_send()

    for source in (ep, near, second, third):
        y_copy(source).wait_send()
        for j in range(1, n_et):
            p_copy(source, lax.rem(et + j, n_et), et).wait_send()


def fused(n_ep, n_et, grad_out, combine, routing, expert_down_matrix, gate_pre, up_pre):
    tokens, feats = grad_out.shape
    hidden, slots = gate_pre.shape[2:]
    cap, half = slots // n_ep, feats // 2
    width = routing.shape[1]
    vmem = pl.BlockSpec(memory_space=pltpu.VMEM)
    dma = pltpu.SemaphoreType.DMA
    gg, ug, gd = pl.pallas_call(
        functools.partial(kernel, n_ep, n_et),
        out_shape=(
            jax.ShapeDtypeStruct((hidden, slots), BF16),
            jax.ShapeDtypeStruct((hidden, slots), BF16),
            jax.ShapeDtypeStruct((half, n_et * hidden), BF16),
        ),
        in_specs=[pl.BlockSpec(memory_space=pltpu.HBM)] * 6,
        out_specs=(vmem, vmem, vmem),
        scratch_shapes=[
            pltpu.VMEM((n_ep, 2, tokens, half), BF16),
            pltpu.VMEM((n_ep, 2, 8, tokens), F32),
            pltpu.VMEM((2, n_ep, cap, half), BF16),
            pltpu.VMEM((2, n_ep, cap, half), BF16),
            pltpu.VMEM((n_ep, cap, half), BF16),
            pltpu.VMEM((n_et, feats, hidden), BF16),
            pltpu.VMEM((2, n_et, slots, hidden), BF16),
            pltpu.VMEM((n_ep, n_et, cap, hidden), BF16),
            pltpu.VMEM((n_ep, n_et, cap, hidden), BF16),
            pltpu.VMEM((n_et, half, hidden), F32),
            pltpu.VMEM((hidden, slots), F32),
            pltpu.VMEM((hidden, slots), F32),
            pltpu.VMEM((slots, hidden), F32),
            pltpu.VMEM((n_et, cap, hidden), F32),
            pltpu.VMEM((width, tokens), F32),
            pltpu.VMEM((width, tokens), jnp.int32),
            pltpu.VMEM((hidden, slots), BF16),
            pltpu.VMEM((hidden, slots), BF16),
            dma((n_et,)),
            dma((6,)),
            dma((n_ep, 2)),
            dma((n_ep, 2)),
            dma((4,)),
            dma((4,)),
            dma((n_ep,)),
            dma((n_ep,)),
            dma((2, n_ep)),
            dma((2, n_ep)),
            dma((n_ep,)),
            dma((n_ep,)),
            dma((7,)),
            dma((7,)),
            dma((n_ep, n_et)),
            dma((n_ep, n_et)),
        ],
        compiler_params=pltpu.CompilerParams(
            collective_id=0, has_side_effects=True, vmem_limit_bytes=60 * 2**20
        ),
    )(grad_out, combine.T, routing.T, expert_down_matrix[0], gate_pre[0, 0], up_pre[0, 0])
    gg, ug, gd = hand_over(gg, ug, gd)
    return gg[None, None], ug[None, None], gd[None]


def hand_over(*arrays):
    pieces = 4

    def copy_kernel(*refs):
        count = len(arrays)
        sems = refs[-1]
        copies = []
        for i in range(count):
            step = arrays[i].shape[0] // pieces
            for j in range(pieces):
                rows = pl.ds(j * step, step)
                copies.append(
                    pltpu.make_async_copy(
                        refs[i].at[rows], refs[count + i].at[rows], sems.at[i, j]
                    )
                )
        for copy in copies:
            copy.start()
        for copy in copies:
            copy.wait()

    anywhere = pl.BlockSpec(memory_space=pl.ANY)
    return pl.pallas_call(
        copy_kernel,
        out_shape=tuple(jax.ShapeDtypeStruct(a.shape, a.dtype) for a in arrays),
        in_specs=[anywhere] * len(arrays),
        out_specs=(anywhere,) * len(arrays),
        scratch_shapes=[pltpu.SemaphoreType.DMA((len(arrays), pieces))],
    )(*arrays)


def plain(n_ep, grad_out, combine, routing, expert_down_matrix, gate_pre, up_pre):
    slot_count = gate_pre.shape[-1]
    cap = slot_count // n_ep
    tokens, feats = grad_out.shape
    width = routing.shape[1]
    pairs = tokens * width
    targets = routing.reshape(pairs)
    onehot = targets[:, None] == jnp.arange(n_ep, dtype=jnp.int32)[None, :]
    place = jnp.arange(pairs, dtype=jnp.int32)
    before = (place[None, :] < place[:, None]).astype(BF16)
    counts = jnp.dot(before, onehot.astype(BF16), preferred_element_type=F32)
    ranking = jnp.sum(jnp.where(onehot, counts, 0.0), axis=1).astype(jnp.int32)
    destination = targets * cap + ranking
    matches = destination[None, :] == jnp.arange(slot_count, dtype=jnp.int32)[:, None]
    filled = jnp.any(matches, axis=1)
    source = jnp.sum(jnp.where(matches, place[None, :], 0), axis=1, dtype=jnp.int32)
    scale = jnp.take(combine.reshape(pairs), source)
    rows = jnp.take(grad_out, source // width, axis=0).astype(F32)
    outgoing = jnp.where(filled[:, None], (rows * scale[:, None]).astype(BF16), jnp.zeros((), BF16))
    incoming = lax.all_to_all(
        outgoing.reshape(n_ep, cap, feats), "ep", split_axis=0, concat_axis=0, tiled=True
    ).reshape(slot_count, feats)
    act_grad = lax.psum_scatter(
        lax.dot_general(
            expert_down_matrix[0], incoming, (((0,), (1,)), ((), ())), preferred_element_type=F32
        ).astype(BF16),
        "et",
        scatter_dimension=0,
        tiled=True,
    ).astype(F32)
    h, u = gate_pre[0, 0].astype(F32), up_pre[0, 0].astype(F32)
    sig = jax.nn.sigmoid(h)
    grad_gate = (act_grad * u * sig * (1.0 + h * (1.0 - sig))).astype(BF16)
    up_grad = (act_grad * h * sig).astype(BF16)
    activation = (h * sig * u).astype(BF16)
    part = lax.dot_general(
        incoming,
        lax.all_gather(activation, "et", axis=0, tiled=True),
        (((0,), (1,)), ((), ())),
        preferred_element_type=F32,
    ).astype(BF16)
    grad_down = lax.psum_scatter(part, "rep", scatter_dimension=0, tiled=True)
    return grad_gate[None, None], up_grad[None, None], grad_down[None]


def solution(mesh):
    n_ep, n_et, n_rep = mesh.shape["ep"], mesh.shape["et"], mesh.shape["rep"]

    def local(grad_out, combine, routing, expert_down_matrix, gate_pre, up_pre):
        args = (grad_out, combine, routing, expert_down_matrix, gate_pre, up_pre)
        whole_tiles = gate_pre.shape[-1] // n_ep % 16 == 0
        if n_ep == 4 and n_et == 4 and n_rep == 2 and whole_tiles:
            return fused(n_ep, n_et, *args)
        return plain(n_ep, *args)

    return jax.shard_map(
        local,
        mesh=mesh,
        in_specs=(
            P(("ep", "rep"), "et"),
            P(("ep", "rep"), None),
            P(("ep", "rep"), None),
            P("ep", "et", None),
            P("ep", "rep", "et", None),
            P("ep", "rep", "et", None),
        ),
        out_specs=(
            P("ep", "rep", "et", None),
            P("ep", "rep", "et", None),
            P("ep", ("et", "rep"), None),
        ),
        check_vma=False,
    )
```

```python
import functools

import jax
import jax.numpy as jnp
from jax import lax
from jax.experimental import pallas as pl
from jax.experimental.pallas import tpu as pltpu
from jax.sharding import PartitionSpec as P

MESH = pl.DeviceIdType.MESH
F32 = jnp.float32
BF16 = jnp.bfloat16


def kernel(
    n_ep, n_et, grad_hbm, comb_hbm, route_hbm, down_ref, gate_hbm, up_hbm,
    gg_ref, ug_ref, gd_ref,
    tok_buf, meta_buf, out_buf, in_buf, y_buf, weight, act_buf, part_buf, sum_buf, total,
    coef_g, coef_u, act_grad, begun, comb_ref, route_ref, gate_ref, up_ref,
    w_sem, l_sem, t_send, t_recv, c_send, c_recv, m_send, m_recv,
    z_send, z_recv, y_send, y_recv, a_send, a_recv, p_send, p_recv,
):
    ep, et, rep = lax.axis_index("ep"), lax.axis_index("et"), lax.axis_index("rep")
    other = 1 - rep
    cap, half = in_buf.shape[2:]
    tokens = tok_buf.shape[2]
    hidden = gate_ref.shape[0]
    across = lax.rem(et + 2, n_et)
    beside = et + 1 - 2 * lax.rem(et, 2)
    last = n_ep - 1
    near = ep + 1 - 2 * lax.rem(ep, 2)
    inner = lax.rem((ep + 1) // 2, 2)
    is_inner = inner == 1
    second = inner * (last - ep) + (1 - inner) * (last - near)
    third = inner * (last - near) + (1 - inner) * (last - ep)
    onward = inner * (last - ep) + (1 - inner) * near

    def load(i):
        if i < 2:
            h = (other, rep)[i]
            columns = pl.ds(pl.multiple_of(h * half, 128), half)
            return pltpu.make_async_copy(grad_hbm.at[:, columns], tok_buf.at[ep, h], l_sem.at[i])
        source, target = (
            (comb_hbm, comb_ref), (route_hbm, route_ref), (gate_hbm, gate_ref), (up_hbm, up_ref)
        )[i - 2]
        return pltpu.make_async_copy(source, target, l_sem.at[i])

    def load_w(t):
        return pltpu.make_async_copy(
            down_ref.at[:, pl.ds(t * hidden, hidden)], weight.at[t], w_sem.at[t]
        )

    barrier = pltpu.get_barrier_semaphore()
    for k in range(1, n_ep):
        pl.semaphore_signal(
            barrier, inc=1, device_id={"ep": lax.rem(ep + k, n_ep)}, device_id_type=MESH
        )
    for k in range(1, n_et):
        pl.semaphore_signal(
            barrier, inc=1, device_id={"et": lax.rem(et + k, n_et)}, device_id_type=MESH
        )
    pl.semaphore_signal(barrier, inc=1, device_id={"rep": other}, device_id_type=MESH)
    for i in (0, 1, 2, 3, 4, 5):
        load(i).start()
    for t in range(n_et):
        load_w(t).start()

    def t_copy(source, h):
        return pltpu.make_async_remote_copy(
            src_ref=tok_buf.at[source, h],
            dst_ref=tok_buf.at[source, h],
            send_sem=t_send.at[source, h],
            recv_sem=t_recv.at[source, h],
            device_id={"ep": onward},
            device_id_type=MESH,
        )

    cuts = (pl.ds(0, half // 256 * 128 + 128), pl.ds(half // 256 * 128 + 128, half - half // 256 * 128 - 128))

    def t_piece(source, j):
        piece = tok_buf.at[source, rep, :, cuts[j]]
        return pltpu.make_async_remote_copy(
            src_ref=piece,
            dst_ref=piece,
            send_sem=c_send.at[j],
            recv_sem=c_recv.at[j],
            device_id={"ep": onward},
            device_id_type=MESH,
        )

    def z_piece(source, j):
        return pltpu.make_async_remote_copy(
            src_ref=out_buf.at[rep, source, :, cuts[j]],
            dst_ref=in_buf.at[rep, source, :, cuts[j]],
            send_sem=c_send.at[2 + j],
            recv_sem=c_recv.at[2 + j],
            device_id={"ep": near},
            device_id_type=MESH,
        )

    def m_copy(source):
        return pltpu.make_async_remote_copy(
            src_ref=meta_buf.at[source],
            dst_ref=meta_buf.at[source],
            send_sem=m_send.at[source],
            recv_sem=m_recv.at[source],
            device_id={"ep": onward},
            device_id_type=MESH,
        )

    def z_copy(source, h):
        return pltpu.make_async_remote_copy(
            src_ref=out_buf.at[h, source],
            dst_ref=in_buf.at[h, source],
            send_sem=z_send.at[h, source],
            recv_sem=z_recv.at[h, source],
            device_id={"ep": near},
            device_id_type=MESH,
        )

    def y_copy(source):
        return pltpu.make_async_remote_copy(
            src_ref=in_buf.at[other, source],
            dst_ref=y_buf.at[source],
            send_sem=y_send.at[source],
            recv_sem=y_recv.at[source],
            device_id={"rep": other},
            device_id_type=MESH,
        )

    def a_copy(i, r, t, target):
        return pltpu.make_async_remote_copy(
            src_ref=act_buf.at[r, t],
            dst_ref=act_buf.at[r, t],
            send_sem=a_send.at[i],
            recv_sem=a_recv.at[i],
            device_id=target,
            device_id_type=MESH,
        )

    def p_copy(source, t, sender):
        return pltpu.make_async_remote_copy(
            src_ref=part_buf.at[source, t],
            dst_ref=sum_buf.at[source, sender],
            send_sem=p_send.at[source, t],
            recv_sem=p_recv.at[source, sender],
            device_id={"et": t},
            device_id_type=MESH,
        )

    pl.semaphore_wait(barrier, n_ep - 1 + n_et - 1 + 1)
    load(0).wait()
    t_copy(ep, other).start()

    load(2).wait()
    load(3).wait()
    rows = meta_buf.shape[2]
    names = lax.broadcasted_iota(jnp.int32, (rows, tokens), 0)
    first = route_ref[0:1, :] == names
    mine = first | (route_ref[1:2, :] == names)
    before = (
        lax.broadcasted_iota(jnp.int32, (tokens, tokens), 0)
        < lax.broadcasted_iota(jnp.int32, (tokens, tokens), 1)
    )
    rank = jnp.dot(
        jnp.where(mine, 1.0, 0.0).astype(BF16),
        jnp.where(before, 1.0, 0.0).astype(BF16),
        preferred_element_type=F32,
    )
    meta_buf[ep, 0] = jnp.where(mine, rank, -1.0)
    meta_buf[ep, 1] = jnp.where(first, comb_ref[0:1, :], comb_ref[1:2, :])
    places = lax.broadcasted_iota(jnp.int32, (cap, tokens), 0).astype(F32)

    def routed(source, h, expert, columns=slice(None)):
        chosen = meta_buf[source, 0, pl.ds(expert, 1), :] == places
        scale = jnp.sum(
            jnp.where(chosen, meta_buf[source, 1, pl.ds(expert, 1), :], 0.0),
            axis=1,
            keepdims=True,
        )
        picked = jnp.dot(
            jnp.where(chosen, 1.0, 0.0).astype(BF16),
            tok_buf[source, h, :, columns],
            preferred_element_type=F32,
        )
        return (picked * scale).astype(BF16)

    m_copy(ep).start()
    load(1).wait()
    t_copy(ep, rep).start()

    def pass_slots(source, h):
        out_buf[h, source] = routed(source, h, near)
        z_copy(source, h).start()

    @pl.when(is_inner)
    def _():
        for h in (other, rep):
            pass_slots(ep, h)

    in_buf[other, ep] = routed(ep, other, ep)
    y_copy(ep).start()
    in_buf[rep, ep] = routed(ep, rep, ep)

    load(4).wait()
    load(5).wait()
    h_value, u_value = gate_ref[...].astype(F32), up_ref[...].astype(F32)
    sig = 1.0 / (1.0 + jnp.exp(-h_value))
    silu = h_value * sig
    act_buf[rep, et] = (silu * u_value).T.astype(BF16)
    to_y, to_x, to_c = {"rep": other}, {"et": across}, {"et": beside}
    a_copy(0, rep, et, to_y).start()
    a_copy(1, rep, et, to_x).start()
    a_copy(3, rep, et, to_c).start()
    coef_g[...] = u_value * sig * (1.0 + h_value * (1.0 - sig))
    coef_u[...] = silu

    def product(h, source, t):
        return jnp.dot(
            in_buf[h, source],
            weight[t, pl.ds(pl.multiple_of(h * half, 128), half)],
            preferred_element_type=F32,
        )

    def begin(source):
        def one(t, carry):
            begun[t] = product(other, source, t)
            return carry

        lax.fori_loop(0, n_et, one, 0)

    def partial(source, is_begun=False):
        def one(k, carry):
            base = et + lax.rem((k + 1) // 2, 2) * (beside - et)
            t = lax.rem(base + 2 * (1 - k // 2), n_et)
            value = product(rep, source, t)
            value = value + (begun[t] if is_begun else product(other, source, t))
            part_buf[source, t] = value.astype(BF16)

            @pl.when(k < n_et - 1)
            def _():
                p_copy(source, t, et).start()

            return carry

        lax.fori_loop(0, n_et, one, 0)

    def weigh(slots_ref, r, source, start=False):
        turned = slots_ref[...].T
        at = pl.multiple_of(source * cap, 16)
        for t in range(n_et):
            value = jnp.dot(
                turned, act_buf[r, t, pl.ds(at, cap), :], preferred_element_type=F32
            )
            total[t] = value if start else total[t] + value

    def weigh_own(source, start=False):
        weigh(in_buf.at[rep, source], rep, source, start)

    def weigh_y(source):
        y_copy(source).wait_recv()
        weigh(y_buf.at[source], other, source)

    def gather(source):
        value = part_buf[source, et].astype(F32)
        for k in range(1, n_et):
            sender = lax.rem(et + k, n_et)
            p_copy(source, et, sender).wait_recv()
            value = value + sum_buf[source, sender].astype(F32)
        act_grad[pl.ds(pl.multiple_of(source * cap, 16), cap), :] = value

    def arrive(which, h):
        source = (near, second, third)[which]

        @pl.when(is_inner)
        def _():
            if h is other:
                m_copy(source).wait_recv()
            t_copy(source, h).wait_recv()
            if which == 0:
                if h is other:
                    m_copy(source).start()
                    t_copy(source, h).start()
                else:
                    for j in range(2):
                        t_piece(source, j).start()
            else:
                pass_slots(source, h)
            in_buf[h, source] = routed(source, h, ep)

        @pl.when(inner == 0)
        def _():
            z_copy(source, h).wait_recv()

        if h is other:
            y_copy(source).start()

    def arrive_last():
        @pl.when(is_inner)
        def _():
            for j in range(2):
                t_piece(third, j).wait_recv()
                out_buf[rep, third, :, cuts[j]] = routed(third, rep, near, cuts[j])
                z_piece(third, j).start()
            in_buf[rep, third] = routed(third, rep, ep)

        @pl.when(inner == 0)
        def _():
            for j in range(2):
                z_piece(third, j).wait_recv()

    for t in range(n_et):
        load_w(t).wait()
    partial(ep)
    arrive(0, other)
    a_copy(0, other, et, to_y).wait_recv()
    a_copy(2, other, et, to_x).start()
    a_copy(4, other, et, to_c).start()
    a_copy(1, rep, across, to_x).wait_recv()
    a_copy(5, rep, across, to_c).start()
    arrive(1, other)
    gather(ep)
    arrive(0, rep)
    a_copy(2, other, across, to_x).wait_recv()
    a_copy(6, other, across, to_c).start()
    partial(near)
    arrive(1, rep)
    partial(second)
    far = lax.rem(beside + 2, n_et)
    a_copy(3, rep, beside, to_c).wait_recv()
    a_copy(4, other, beside, to_c).wait_recv()
    a_copy(5, rep, far, to_c).wait_recv()
    a_copy(6, other, far, to_c).wait_recv()
    weigh_own(ep, True)
    weigh_y(ep)
    weigh_own(near)
    gather(near)
    arrive(2, other)
    weigh_y(near)
    weigh_own(second)
    gather(second)
    begin(third)
    arrive_last()
    partial(third, True)
    weigh_y(second)
    weigh_own(third)
    weigh_y(third)
    for t in range(n_et):
        gd_ref[:, pl.ds(t * hidden, hidden)] = total[t].astype(BF16)
    gather(third)
    value = act_grad[...].T
    gg_ref[...] = (value * coef_g[...]).astype(BF16)
    ug_ref[...] = (value * coef_u[...]).astype(BF16)

    for i, (r, t, target) in enumerate((
        (rep, et, to_y), (rep, et, to_x), (other, et, to_x),
        (rep, et, to_c), (other, et, to_c), (rep, across, to_c), (other, across, to_c),
    )):
        a_copy(i, r, t, target).wait_send()
    m_copy(ep).wait_send()
    for h in (other, rep):
        t_copy(ep, h).wait_send()

    @pl.when(is_inner)
    def _():
        m_copy(near).wait_send()
        for h in (other, rep):
            for source in (ep, second):
                z_copy(source, h).wait_send()
        t_copy(near, other).wait_send()
        z_copy(third, other).wait_send()
        for j in range(2):
            t_piece(near, j).wait_send()
            z_piece(third, j).wait_send()

    for source in (ep, near, second, third):
        y_copy(source).wait_send()
        for j in range(1, n_et):
            p_copy(source, lax.rem(et + j, n_et), et).wait_send()


def fused(n_ep, n_et, grad_out, combine, routing, expert_down_matrix, gate_pre, up_pre):
    tokens, feats = grad_out.shape
    hidden, slots = gate_pre.shape[2:]
    cap, half = slots // n_ep, feats // 2
    width = routing.shape[1]
    vmem = pl.BlockSpec(memory_space=pltpu.VMEM)
    dma = pltpu.SemaphoreType.DMA
    gg, ug, gd = pl.pallas_call(
        functools.partial(kernel, n_ep, n_et),
        out_shape=(
            jax.ShapeDtypeStruct((hidden, slots), BF16),
            jax.ShapeDtypeStruct((hidden, slots), BF16),
            jax.ShapeDtypeStruct((half, n_et * hidden), BF16),
        ),
        in_specs=[pl.BlockSpec(memory_space=pltpu.HBM)] * 6,
        out_specs=(vmem, vmem, vmem),
        scratch_shapes=[
            pltpu.VMEM((n_ep, 2, tokens, half), BF16),
            pltpu.VMEM((n_ep, 2, 8, tokens), F32),
            pltpu.VMEM((2, n_ep, cap, half), BF16),
            pltpu.VMEM((2, n_ep, cap, half), BF16),
            pltpu.VMEM((n_ep, cap, half), BF16),
            pltpu.VMEM((n_et, feats, hidden), BF16),
            pltpu.VMEM((2, n_et, slots, hidden), BF16),
            pltpu.VMEM((n_ep, n_et, cap, hidden), BF16),
            pltpu.VMEM((n_ep, n_et, cap, hidden), BF16),
            pltpu.VMEM((n_et, half, hidden), F32),
            pltpu.VMEM((hidden, slots), F32),
            pltpu.VMEM((hidden, slots), F32),
            pltpu.VMEM((slots, hidden), F32),
            pltpu.VMEM((n_et, cap, hidden), F32),
            pltpu.VMEM((width, tokens), F32),
            pltpu.VMEM((width, tokens), jnp.int32),
            pltpu.VMEM((hidden, slots), BF16),
            pltpu.VMEM((hidden, slots), BF16),
            dma((n_et,)),
            dma((6,)),
            dma((n_ep, 2)),
            dma((n_ep, 2)),
            dma((4,)),
            dma((4,)),
            dma((n_ep,)),
            dma((n_ep,)),
            dma((2, n_ep)),
            dma((2, n_ep)),
            dma((n_ep,)),
            dma((n_ep,)),
            dma((7,)),
            dma((7,)),
            dma((n_ep, n_et)),
            dma((n_ep, n_et)),
        ],
        compiler_params=pltpu.CompilerParams(
            collective_id=0, has_side_effects=True, vmem_limit_bytes=60 * 2**20
        ),
    )(grad_out, combine.T, routing.T, expert_down_matrix[0], gate_pre[0, 0], up_pre[0, 0])
    gg, ug, gd = hand_over(gg, ug, gd)
    return gg[None, None], ug[None, None], gd[None]


def hand_over(*arrays):
    pieces = 4

    def copy_kernel(*refs):
        count = len(arrays)
        taken, given, held = refs[:count], refs[count:2 * count], refs[2 * count:3 * count]
        in_sems, out_sems = refs[3 * count:]
        loads, stores = [], []
        for i in range(count):
            step = arrays[i].shape[0] // pieces
            for j in range(pieces):
                rows = pl.ds(j * step, step)
                loads.append(
                    pltpu.make_async_copy(taken[i].at[rows], held[i].at[rows], in_sems.at[i, j])
                )
                stores.append(
                    pltpu.make_async_copy(held[i].at[rows], given[i].at[rows], out_sems.at[i, j])
                )
        for load in loads:
            load.start()
        for load, store in zip(loads, stores):
            load.wait()
            store.start()
        for store in stores:
            store.wait()

    far = pl.BlockSpec(memory_space=pltpu.HBM)
    sems = pltpu.SemaphoreType.DMA((len(arrays), pieces))
    return pl.pallas_call(
        copy_kernel,
        out_shape=tuple(jax.ShapeDtypeStruct(a.shape, a.dtype) for a in arrays),
        in_specs=[far] * len(arrays),
        out_specs=(far,) * len(arrays),
        scratch_shapes=[pltpu.VMEM(a.shape, a.dtype) for a in arrays] + [sems, sems],
        compiler_params=pltpu.CompilerParams(vmem_limit_bytes=60 * 2**20),
    )(*arrays)


def plain(n_ep, grad_out, combine, routing, expert_down_matrix, gate_pre, up_pre):
    slot_count = gate_pre.shape[-1]
    cap = slot_count // n_ep
    tokens, feats = grad_out.shape
    width = routing.shape[1]
    pairs = tokens * width
    targets = routing.reshape(pairs)
    onehot = targets[:, None] == jnp.arange(n_ep, dtype=jnp.int32)[None, :]
    place = jnp.arange(pairs, dtype=jnp.int32)
    before = (place[None, :] < place[:, None]).astype(BF16)
    counts = jnp.dot(before, onehot.astype(BF16), preferred_element_type=F32)
    ranking = jnp.sum(jnp.where(onehot, counts, 0.0), axis=1).astype(jnp.int32)
    destination = targets * cap + ranking
    matches = destination[None, :] == jnp.arange(slot_count, dtype=jnp.int32)[:, None]
    filled = jnp.any(matches, axis=1)
    source = jnp.sum(jnp.where(matches, place[None, :], 0), axis=1, dtype=jnp.int32)
    scale = jnp.take(combine.reshape(pairs), source)
    rows = jnp.take(grad_out, source // width, axis=0).astype(F32)
    outgoing = jnp.where(filled[:, None], (rows * scale[:, None]).astype(BF16), jnp.zeros((), BF16))
    incoming = lax.all_to_all(
        outgoing.reshape(n_ep, cap, feats), "ep", split_axis=0, concat_axis=0, tiled=True
    ).reshape(slot_count, feats)
    act_grad = lax.psum_scatter(
        lax.dot_general(
            expert_down_matrix[0], incoming, (((0,), (1,)), ((), ())), preferred_element_type=F32
        ).astype(BF16),
        "et",
        scatter_dimension=0,
        tiled=True,
    ).astype(F32)
    h, u = gate_pre[0, 0].astype(F32), up_pre[0, 0].astype(F32)
    sig = jax.nn.sigmoid(h)
    grad_gate = (act_grad * u * sig * (1.0 + h * (1.0 - sig))).astype(BF16)
    up_grad = (act_grad * h * sig).astype(BF16)
    activation = (h * sig * u).astype(BF16)
    part = lax.dot_general(
        incoming,
        lax.all_gather(activation, "et", axis=0, tiled=True),
        (((0,), (1,)), ((), ())),
        preferred_element_type=F32,
    ).astype(BF16)
    grad_down = lax.psum_scatter(part, "rep", scatter_dimension=0, tiled=True)
    return grad_gate[None, None], up_grad[None, None], grad_down[None]


def solution(mesh):
    n_ep, n_et, n_rep = mesh.shape["ep"], mesh.shape["et"], mesh.shape["rep"]

    def local(grad_out, combine, routing, expert_down_matrix, gate_pre, up_pre):
        args = (grad_out, combine, routing, expert_down_matrix, gate_pre, up_pre)
        whole_tiles = gate_pre.shape[-1] // n_ep % 16 == 0
        if n_ep == 4 and n_et == 4 and n_rep == 2 and whole_tiles:
            return fused(n_ep, n_et, *args)
        return plain(n_ep, *args)

    return jax.shard_map(
        local,
        mesh=mesh,
        in_specs=(
            P(("ep", "rep"), "et"),
            P(("ep", "rep"), None),
            P(("ep", "rep"), None),
            P("ep", "et", None),
            P("ep", "rep", "et", None),
            P("ep", "rep", "et", None),
        ),
        out_specs=(
            P("ep", "rep", "et", None),
            P("ep", "rep", "et", None),
            P("ep", ("et", "rep"), None),
        ),
        check_vma=False,
    )
```

```python
import functools

import jax
import jax.numpy as jnp
from jax import lax
from jax.experimental import pallas as pl
from jax.experimental.pallas import tpu as pltpu
from jax.sharding import PartitionSpec as P

MESH = pl.DeviceIdType.MESH
F32 = jnp.float32
BF16 = jnp.bfloat16


def kernel(
    n_ep, n_et, grad_hbm, comb_hbm, route_hbm, down_ref, gate_hbm, up_hbm,
    gg_ref, ug_ref, gd_ref,
    tok_buf, meta_buf, out_buf, in_buf, y_buf, weight, act_buf, part_buf, sum_buf, total,
    coef_g, coef_u, act_grad, begun, comb_ref, route_ref, gate_ref, up_ref,
    w_sem, l_sem, t_send, t_recv, m_send, m_recv,
    z_send, z_recv, y_send, y_recv, a_send, a_recv, p_send, p_recv,
):
    ep, et, rep = lax.axis_index("ep"), lax.axis_index("et"), lax.axis_index("rep")
    other = 1 - rep
    cap, half = in_buf.shape[2:]
    tokens = tok_buf.shape[2]
    hidden = gate_ref.shape[0]
    across = lax.rem(et + 2, n_et)
    beside = et + 1 - 2 * lax.rem(et, 2)
    last = n_ep - 1
    near = ep + 1 - 2 * lax.rem(ep, 2)
    inner = lax.rem((ep + 1) // 2, 2)
    is_inner = inner == 1
    second = inner * (last - ep) + (1 - inner) * (last - near)
    third = inner * (last - near) + (1 - inner) * (last - ep)
    onward = inner * (last - ep) + (1 - inner) * near

    def load(i):
        if i < 2:
            h = (other, rep)[i]
            columns = pl.ds(pl.multiple_of(h * half, 128), half)
            return pltpu.make_async_copy(grad_hbm.at[:, columns], tok_buf.at[ep, h], l_sem.at[i])
        source, target = (
            (comb_hbm, comb_ref), (route_hbm, route_ref), (gate_hbm, gate_ref), (up_hbm, up_ref)
        )[i - 2]
        return pltpu.make_async_copy(source, target, l_sem.at[i])

    def load_w(t):
        return pltpu.make_async_copy(
            down_ref.at[:, pl.ds(t * hidden, hidden)], weight.at[t], w_sem.at[t]
        )

    barrier = pltpu.get_barrier_semaphore()
    for k in range(1, n_ep):
        pl.semaphore_signal(
            barrier, inc=1, device_id={"ep": lax.rem(ep + k, n_ep)}, device_id_type=MESH
        )
    for k in range(1, n_et):
        pl.semaphore_signal(
            barrier, inc=1, device_id={"et": lax.rem(et + k, n_et)}, device_id_type=MESH
        )
    pl.semaphore_signal(barrier, inc=1, device_id={"rep": other}, device_id_type=MESH)
    for i in (0, 1, 2, 3, 4, 5):
        load(i).start()
    for t in range(n_et):
        load_w(t).start()

    def t_copy(source, h):
        return pltpu.make_async_remote_copy(
            src_ref=tok_buf.at[source, h],
            dst_ref=tok_buf.at[source, h],
            send_sem=t_send.at[source, h],
            recv_sem=t_recv.at[source, h],
            device_id={"ep": onward},
            device_id_type=MESH,
        )

    def m_copy(source):
        return pltpu.make_async_remote_copy(
            src_ref=meta_buf.at[source],
            dst_ref=meta_buf.at[source],
            send_sem=m_send.at[source],
            recv_sem=m_recv.at[source],
            device_id={"ep": onward},
            device_id_type=MESH,
        )

    def z_copy(source, h):
        return pltpu.make_async_remote_copy(
            src_ref=out_buf.at[h, source],
            dst_ref=in_buf.at[h, source],
            send_sem=z_send.at[h, source],
            recv_sem=z_recv.at[h, source],
            device_id={"ep": near},
            device_id_type=MESH,
        )

    def y_copy(source):
        return pltpu.make_async_remote_copy(
            src_ref=in_buf.at[other, source],
            dst_ref=y_buf.at[source],
            send_sem=y_send.at[source],
            recv_sem=y_recv.at[source],
            device_id={"rep": other},
            device_id_type=MESH,
        )

    def a_copy(i, r, t, target):
        return pltpu.make_async_remote_copy(
            src_ref=act_buf.at[r, t],
            dst_ref=act_buf.at[r, t],
            send_sem=a_send.at[i],
            recv_sem=a_recv.at[i],
            device_id=target,
            device_id_type=MESH,
        )

    def p_copy(source, t, sender):
        return pltpu.make_async_remote_copy(
            src_ref=part_buf.at[source, t],
            dst_ref=sum_buf.at[source, sender],
            send_sem=p_send.at[source, t],
            recv_sem=p_recv.at[source, sender],
            device_id={"et": t},
            device_id_type=MESH,
        )

    pl.semaphore_wait(barrier, n_ep - 1 + n_et - 1 + 1)
    load(0).wait()
    t_copy(ep, other).start()

    load(2).wait()
    load(3).wait()
    rows = meta_buf.shape[2]
    names = lax.broadcasted_iota(jnp.int32, (rows, tokens), 0)
    first = route_ref[0:1, :] == names
    mine = first | (route_ref[1:2, :] == names)
    before = (
        lax.broadcasted_iota(jnp.int32, (tokens, tokens), 0)
        < lax.broadcasted_iota(jnp.int32, (tokens, tokens), 1)
    )
    rank = jnp.dot(
        jnp.where(mine, 1.0, 0.0).astype(BF16),
        jnp.where(before, 1.0, 0.0).astype(BF16),
        preferred_element_type=F32,
    )
    meta_buf[ep, 0] = jnp.where(mine, rank, -1.0)
    meta_buf[ep, 1] = jnp.where(first, comb_ref[0:1, :], comb_ref[1:2, :])
    places = lax.broadcasted_iota(jnp.int32, (cap, tokens), 0).astype(F32)

    def routed(source, h, expert, columns=slice(None)):
        chosen = meta_buf[source, 0, pl.ds(expert, 1), :] == places
        scale = jnp.sum(
            jnp.where(chosen, meta_buf[source, 1, pl.ds(expert, 1), :], 0.0),
            axis=1,
            keepdims=True,
        )
        picked = jnp.dot(
            jnp.where(chosen, 1.0, 0.0).astype(BF16),
            tok_buf[source, h, :, columns],
            preferred_element_type=F32,
        )
        return (picked * scale).astype(BF16)

    m_copy(ep).start()
    load(1).wait()
    t_copy(ep, rep).start()

    def pass_slots(source, h):
        out_buf[h, source] = routed(source, h, near)
        z_copy(source, h).start()

    @pl.when(is_inner)
    def _():
        for h in (other, rep):
            pass_slots(ep, h)

    in_buf[other, ep] = routed(ep, other, ep)
    y_copy(ep).start()
    in_buf[rep, ep] = routed(ep, rep, ep)

    load(4).wait()
    load(5).wait()
    h_value, u_value = gate_ref[...].astype(F32), up_ref[...].astype(F32)
    sig = 1.0 / (1.0 + jnp.exp(-h_value))
    silu = h_value * sig
    act_buf[rep, et] = (silu * u_value).T.astype(BF16)
    to_y, to_x, to_c = {"rep": other}, {"et": across}, {"et": beside}
    a_copy(0, rep, et, to_y).start()
    a_copy(1, rep, et, to_x).start()
    a_copy(3, rep, et, to_c).start()
    coef_g[...] = u_value * sig * (1.0 + h_value * (1.0 - sig))
    coef_u[...] = silu

    def product(h, source, t):
        return jnp.dot(
            in_buf[h, source],
            weight[t, pl.ds(pl.multiple_of(h * half, 128), half)],
            preferred_element_type=F32,
        )

    def begin(source):
        def one(t, carry):
            begun[t] = product(other, source, t)
            return carry

        lax.fori_loop(0, n_et, one, 0)

    def partial(source, is_begun=False):
        def one(k, carry):
            base = et + lax.rem((k + 1) // 2, 2) * (beside - et)
            t = lax.rem(base + 2 * (1 - k // 2), n_et)
            value = product(rep, source, t)
            value = value + (begun[t] if is_begun else product(other, source, t))
            part_buf[source, t] = value.astype(BF16)

            @pl.when(k < n_et - 1)
            def _():
                p_copy(source, t, et).start()

            return carry

        lax.fori_loop(0, n_et, one, 0)

    def weigh(slots_ref, r, source, start=False):
        turned = slots_ref[...].T
        at = pl.multiple_of(source * cap, 16)
        for t in range(n_et):
            value = jnp.dot(
                turned, act_buf[r, t, pl.ds(at, cap), :], preferred_element_type=F32
            )
            total[t] = value if start else total[t] + value

    def weigh_own(source, start=False):
        weigh(in_buf.at[rep, source], rep, source, start)

    def weigh_y(source):
        y_copy(source).wait_recv()
        weigh(y_buf.at[source], other, source)

    def gather(source):
        value = part_buf[source, et].astype(F32)
        for k in range(1, n_et):
            sender = lax.rem(et + k, n_et)
            p_copy(source, et, sender).wait_recv()
            value = value + sum_buf[source, sender].astype(F32)
        act_grad[pl.ds(pl.multiple_of(source * cap, 16), cap), :] = value

    def arrive(which, h):
        source = (near, second, third)[which]

        @pl.when(is_inner)
        def _():
            if h is other:
                m_copy(source).wait_recv()
            t_copy(source, h).wait_recv()
            if which == 0:
                if h is other:
                    m_copy(source).start()
                t_copy(source, h).start()
            else:
                pass_slots(source, h)
            in_buf[h, source] = routed(source, h, ep)

        @pl.when(inner == 0)
        def _():
            z_copy(source, h).wait_recv()

        if h is other:
            y_copy(source).start()

    for t in range(n_et):
        load_w(t).wait()
    partial(ep)
    arrive(0, other)
    a_copy(0, other, et, to_y).wait_recv()
    a_copy(2, other, et, to_x).start()
    a_copy(4, other, et, to_c).start()
    a_copy(1, rep, across, to_x).wait_recv()
    a_copy(5, rep, across, to_c).start()
    arrive(1, other)
    gather(ep)
    arrive(0, rep)
    a_copy(2, other, across, to_x).wait_recv()
    a_copy(6, other, across, to_c).start()
    partial(near)
    arrive(1, rep)
    partial(second)
    far = lax.rem(beside + 2, n_et)
    a_copy(3, rep, beside, to_c).wait_recv()
    a_copy(4, other, beside, to_c).wait_recv()
    a_copy(5, rep, far, to_c).wait_recv()
    a_copy(6, other, far, to_c).wait_recv()
    weigh_own(ep, True)
    weigh_y(ep)
    weigh_own(near)
    gather(near)
    arrive(2, other)
    weigh_y(near)
    weigh_own(second)
    gather(second)
    begin(third)
    arrive(2, rep)
    partial(third, True)
    weigh_y(second)
    weigh_own(third)
    weigh_y(third)
    for t in range(n_et):
        gd_ref[:, pl.ds(t * hidden, hidden)] = total[t].astype(BF16)
    gather(third)
    value = act_grad[...].T
    gg_ref[...] = (value * coef_g[...]).astype(BF16)
    ug_ref[...] = (value * coef_u[...]).astype(BF16)

    for i, (r, t, target) in enumerate((
        (rep, et, to_y), (rep, et, to_x), (other, et, to_x),
        (rep, et, to_c), (other, et, to_c), (rep, across, to_c), (other, across, to_c),
    )):
        a_copy(i, r, t, target).wait_send()
    m_copy(ep).wait_send()
    for h in (other, rep):
        t_copy(ep, h).wait_send()

    @pl.when(is_inner)
    def _():
        m_copy(near).wait_send()
        for h in (other, rep):
            t_copy(near, h).wait_send()
            for source in (ep, second, third):
                z_copy(source, h).wait_send()

    for source in (ep, near, second, third):
        y_copy(source).wait_send()
        for j in range(1, n_et):
            p_copy(source, lax.rem(et + j, n_et), et).wait_send()


def fused(n_ep, n_et, grad_out, combine, routing, expert_down_matrix, gate_pre, up_pre):
    tokens, feats = grad_out.shape
    hidden, slots = gate_pre.shape[2:]
    cap, half = slots // n_ep, feats // 2
    width = routing.shape[1]
    vmem = pl.BlockSpec(memory_space=pltpu.VMEM)
    dma = pltpu.SemaphoreType.DMA
    gg, ug, gd = pl.pallas_call(
        functools.partial(kernel, n_ep, n_et),
        out_shape=(
            jax.ShapeDtypeStruct((hidden, slots), BF16),
            jax.ShapeDtypeStruct((hidden, slots), BF16),
            jax.ShapeDtypeStruct((half, n_et * hidden), BF16),
        ),
        in_specs=[pl.BlockSpec(memory_space=pltpu.HBM)] * 6,
        out_specs=(vmem, vmem, vmem),
        scratch_shapes=[
            pltpu.VMEM((n_ep, 2, tokens, half), BF16),
            pltpu.VMEM((n_ep, 2, 8, tokens), F32),
            pltpu.VMEM((2, n_ep, cap, half), BF16),
            pltpu.VMEM((2, n_ep, cap, half), BF16),
            pltpu.VMEM((n_ep, cap, half), BF16),
            pltpu.VMEM((n_et, feats, hidden), BF16),
            pltpu.VMEM((2, n_et, slots, hidden), BF16),
            pltpu.VMEM((n_ep, n_et, cap, hidden), BF16),
            pltpu.VMEM((n_ep, n_et, cap, hidden), BF16),
            pltpu.VMEM((n_et, half, hidden), F32),
            pltpu.VMEM((hidden, slots), F32),
            pltpu.VMEM((hidden, slots), F32),
            pltpu.VMEM((slots, hidden), F32),
            pltpu.VMEM((n_et, cap, hidden), F32),
            pltpu.VMEM((width, tokens), F32),
            pltpu.VMEM((width, tokens), jnp.int32),
            pltpu.VMEM((hidden, slots), BF16),
            pltpu.VMEM((hidden, slots), BF16),
            dma((n_et,)),
            dma((6,)),
            dma((n_ep, 2)),
            dma((n_ep, 2)),
            dma((n_ep,)),
            dma((n_ep,)),
            dma((2, n_ep)),
            dma((2, n_ep)),
            dma((n_ep,)),
            dma((n_ep,)),
            dma((7,)),
            dma((7,)),
            dma((n_ep, n_et)),
            dma((n_ep, n_et)),
        ],
        compiler_params=pltpu.CompilerParams(
            collective_id=0, has_side_effects=True, vmem_limit_bytes=60 * 2**20
        ),
    )(grad_out, combine.T, routing.T, expert_down_matrix[0], gate_pre[0, 0], up_pre[0, 0])
    gg, ug, gd = hand_over(gg, ug, gd)
    return gg[None, None], ug[None, None], gd[None]


def hand_over(*arrays):
    pieces = 4

    def copy_kernel(*refs):
        count = len(arrays)
        taken, given, held = refs[:count], refs[count:2 * count], refs[2 * count:3 * count]
        in_sems, out_sems = refs[3 * count:]
        loads, stores = [], []
        for i in range(count):
            step = arrays[i].shape[0] // pieces
            for j in range(pieces):
                rows = pl.ds(j * step, step)
                loads.append(
                    pltpu.make_async_copy(taken[i].at[rows], held[i].at[rows], in_sems.at[i, j])
                )
                stores.append(
                    pltpu.make_async_copy(held[i].at[rows], given[i].at[rows], out_sems.at[i, j])
                )
        for load in loads:
            load.start()
        for load, store in zip(loads, stores):
            load.wait()
            store.start()
        for store in stores:
            store.wait()

    far = pl.BlockSpec(memory_space=pltpu.HBM)
    sems = pltpu.SemaphoreType.DMA((len(arrays), pieces))
    return pl.pallas_call(
        copy_kernel,
        out_shape=tuple(jax.ShapeDtypeStruct(a.shape, a.dtype) for a in arrays),
        in_specs=[far] * len(arrays),
        out_specs=(far,) * len(arrays),
        scratch_shapes=[pltpu.VMEM(a.shape, a.dtype) for a in arrays] + [sems, sems],
        compiler_params=pltpu.CompilerParams(vmem_limit_bytes=60 * 2**20),
    )(*arrays)


def plain(n_ep, grad_out, combine, routing, expert_down_matrix, gate_pre, up_pre):
    slot_count = gate_pre.shape[-1]
    cap = slot_count // n_ep
    tokens, feats = grad_out.shape
    width = routing.shape[1]
    pairs = tokens * width
    targets = routing.reshape(pairs)
    onehot = targets[:, None] == jnp.arange(n_ep, dtype=jnp.int32)[None, :]
    place = jnp.arange(pairs, dtype=jnp.int32)
    before = (place[None, :] < place[:, None]).astype(BF16)
    counts = jnp.dot(before, onehot.astype(BF16), preferred_element_type=F32)
    ranking = jnp.sum(jnp.where(onehot, counts, 0.0), axis=1).astype(jnp.int32)
    destination = targets * cap + ranking
    matches = destination[None, :] == jnp.arange(slot_count, dtype=jnp.int32)[:, None]
    filled = jnp.any(matches, axis=1)
    source = jnp.sum(jnp.where(matches, place[None, :], 0), axis=1, dtype=jnp.int32)
    scale = jnp.take(combine.reshape(pairs), source)
    rows = jnp.take(grad_out, source // width, axis=0).astype(F32)
    outgoing = jnp.where(filled[:, None], (rows * scale[:, None]).astype(BF16), jnp.zeros((), BF16))
    incoming = lax.all_to_all(
        outgoing.reshape(n_ep, cap, feats), "ep", split_axis=0, concat_axis=0, tiled=True
    ).reshape(slot_count, feats)
    act_grad = lax.psum_scatter(
        lax.dot_general(
            expert_down_matrix[0], incoming, (((0,), (1,)), ((), ())), preferred_element_type=F32
        ).astype(BF16),
        "et",
        scatter_dimension=0,
        tiled=True,
    ).astype(F32)
    h, u = gate_pre[0, 0].astype(F32), up_pre[0, 0].astype(F32)
    sig = jax.nn.sigmoid(h)
    grad_gate = (act_grad * u * sig * (1.0 + h * (1.0 - sig))).astype(BF16)
    up_grad = (act_grad * h * sig).astype(BF16)
    activation = (h * sig * u).astype(BF16)
    part = lax.dot_general(
        incoming,
        lax.all_gather(activation, "et", axis=0, tiled=True),
        (((0,), (1,)), ((), ())),
        preferred_element_type=F32,
    ).astype(BF16)
    grad_down = lax.psum_scatter(part, "rep", scatter_dimension=0, tiled=True)
    return grad_gate[None, None], up_grad[None, None], grad_down[None]


def solution(mesh):
    n_ep, n_et, n_rep = mesh.shape["ep"], mesh.shape["et"], mesh.shape["rep"]

    def local(grad_out, combine, routing, expert_down_matrix, gate_pre, up_pre):
        args = (grad_out, combine, routing, expert_down_matrix, gate_pre, up_pre)
        whole_tiles = gate_pre.shape[-1] // n_ep % 16 == 0
        if n_ep == 4 and n_et == 4 and n_rep == 2 and whole_tiles:
            return fused(n_ep, n_et, *args)
        return plain(n_ep, *args)

    return jax.shard_map(
        local,
        mesh=mesh,
        in_specs=(
            P(("ep", "rep"), "et"),
            P(("ep", "rep"), None),
            P(("ep", "rep"), None),
            P("ep", "et", None),
            P("ep", "rep", "et", None),
            P("ep", "rep", "et", None),
        ),
        out_specs=(
            P("ep", "rep", "et", None),
            P("ep", "rep", "et", None),
            P("ep", ("et", "rep"), None),
        ),
        check_vma=False,
    )
```
